512 devices in a mesh: ctx: 32 (over y, x, core), tp: 16 (over z).
Axes of the slice: x: 4, y: 4, z: 16, core: 2. Of those that a mesh axis runs over, the one named last changes fastest.
Arguments:
- hidden: bfloat16 [2, 4096, 4096], P(None, 'ctx', 'tp'), may hold values from -6 to 6
- norm_gain: float32 [4096], replicated, may hold values from 0.5 to 1.5
- in_weight: bfloat16 [4096, 3, 4096], P('ctx', None, 'tp'), may hold values from -0.09375 to 0.09375
- short_weight: float32 [3, 3, 4096], P(None, None, 'tp'), may hold values from -4 to 4
- residues: float32 [16, 4096], P(None, 'tp'), may hold values from -5 to 5
- rates: float32 [16, 4096], P(None, 'tp'), may hold values from 7.324219e-05 to 0.05
- skip_gain: float32 [4096], P('tp'), may hold values from -4 to 4
- out_weight: bfloat16 [4096, 4096], P('tp', 'ctx'), may hold values from -0.09375 to 0.09375
- lengths: int32 [2], replicated, may hold values from 512 to 4096, as said below
Outputs:
- block_out: bfloat16 [2, 4096, 4096], P(None, 'ctx', 'tp')
The draws below stay inside these ranges and needn't reach their ends.
Inputs may be any that keep to these rules, and one draw needn't show every extreme that they name: `lengths`: one of the 2 sequences, drawn from the seed, has all 4096 positions valid; the other has between 512 and 4096.
All inputs are finite; a program needn't handle non-finite values.
Results may differ from the reference program's by a relative error of at most 0.023.
Values may be sent and summed in bfloat16 or wider, within the bound.
A program may use at most 128 MiB of HBM per device.

```python
import math
import jax
import jax.numpy as jnp
from jax import lax

D = 4096
MODES = 16
SHORT = 3
SAMPLES = 2
SEQ = 4096
N_TP = 16


def draw_lengths(key, part):
    key = jax.random.fold_in(key, 7)
    first, second = jax.random.split(key)
    full_one = jax.random.randint(first, (), 0, SAMPLES)
    others = jax.random.randint(second, (SAMPLES,), SEQ // 8, SEQ + 1)
    return jnp.where(jnp.arange(SAMPLES) == full_one, SEQ, others).astype(jnp.int32)


def level_of(rng, dims, cuts, smallest, top_value):
    factor_of, own = 1.0, jax.random.fold_in(rng, 6)
    for position, parts in cuts:
        steps = jnp.exp(jax.random.uniform(jax.random.fold_in(own, position), (parts,), jnp.float32, smallest / len(cuts), top_value / len(cuts)))
        factor_of = factor_of * jnp.repeat(steps, dims[position] // parts).reshape([-1 if axis == position else 1 for axis in range(len(dims))])
    return factor_of


def gaussian(stream_key, dims, spread, most, shards=(), kind=jnp.bfloat16):
    result = spread * jax.random.normal(stream_key, dims, jnp.float32)
    if shards:
        result = result * level_of(stream_key, dims, shards, -0.22, 0.18)
    return jnp.clip(result, -most, most).astype(kind)


def setup_inputs(seed: int = 0) -> dict:
    key_of = jax.random.split(jax.random.key(seed), 10)
    hidden = gaussian(key_of[0], (SAMPLES, SEQ, D), 1.0, 6.0, ((1, 32), (2, 16)))
    norm_gain = jnp.clip(1.0 + 0.1 * jax.random.normal(key_of[1], (D,), jnp.float32), 0.5, 1.5)
    in_weight = gaussian(key_of[2], (D, 3, D), D ** -0.5, 0.09375, ((0, 32), (2, 16)))
    short_weight = gaussian(key_of[3], (SHORT, 3, D), 0.6, 4.0, ((2, 16),), jnp.float32)
    residues = gaussian(key_of[4], (MODES, D), 1.0, 5.0, ((1, 16),), jnp.float32)
    rates = jnp.clip(jnp.exp(math.log(0.05) - 6.5260067 * jax.random.uniform(key_of[5], (MODES, D), jnp.float32) ** level_of(key_of[5], (MODES, D), ((1, 16),), -0.2, 0.2)), 7.324219041038305e-05, 0.05)
    skip_gain = gaussian(key_of[6], (D,), 1.0, 4.0, ((0, 16),), jnp.float32)
    out_weight = gaussian(key_of[7], (D, D), D ** -0.5, 0.09375, ((0, 16), (1, 32)))
    lengths = draw_lengths(jax.random.fold_in(key_of[9], 71), 0)
    return {"hidden": hidden, "norm_gain": norm_gain, "in_weight": in_weight, "short_weight": short_weight, "residues": residues, "rates": rates, "skip_gain": skip_gain, "out_weight": out_weight, "lengths": lengths}


def reference(hidden, norm_gain, in_weight, short_weight, residues, rates, skip_gain, out_weight, lengths):
    xf = hidden.astype(jnp.float32)
    scale = lax.rsqrt(lax.optimization_barrier(jnp.mean(xf * xf, axis=-1, keepdims=True)) + 1e-06)
    normed = (xf * scale * norm_gain).astype(jnp.bfloat16)
    proj = jnp.dot(normed.reshape(SAMPLES * SEQ, D), in_weight.reshape(D, 3 * D), preferred_element_type=jnp.float32)
    proj = proj.astype(jnp.bfloat16).reshape(SAMPLES, SEQ, 3, D).astype(jnp.float32)
    padded = jnp.pad(proj, ((0, 0), (SHORT - 1, 0), (0, 0), (0, 0)))
    feat = jnp.zeros_like(proj)
    for i in range(SHORT):
        feat = feat + short_weight[i] * padded[:, SHORT - 1 - i:SHORT - 1 - i + SEQ]
    query, keys, values = (feat[:, :, 0], feat[:, :, 1], feat[:, :, 2])
    positions = jnp.arange(SEQ, dtype=jnp.int32)
    valid = (positions[None, :] < lengths[:, None]).astype(jnp.float32)[..., None]
    inputs = (keys * values * valid).astype(jnp.bfloat16).astype(jnp.float32)
    coef = residues * jnp.sqrt(2.0 * rates / MODES)
    decay = jnp.exp(-rates)

    def advance(state, column):
        state = decay[None] * state + column[:, None, :]
        return (state, lax.optimization_barrier(jnp.sum(coef[None] * state, axis=1)))
    start = jnp.zeros((SAMPLES, MODES, D), jnp.float32)
    _, conv = lax.scan(advance, start, jnp.transpose(inputs, (1, 0, 2)))
    conv = jnp.transpose(conv, (1, 0, 2))
    gated = (query * (conv + skip_gain * inputs) * valid).astype(jnp.bfloat16)
    flat = gated.reshape(SAMPLES * SEQ, N_TP, D // N_TP)
    weights = out_weight.reshape(N_TP, D // N_TP, D)

    def add_group(total, group):
        part = jnp.dot(flat[:, group], weights[group], preferred_element_type=jnp.float32)
        part = lax.optimization_barrier(part.astype(jnp.bfloat16))
        return (total + part.astype(jnp.float32), None)
    total, _ = lax.scan(add_group, jnp.zeros((SAMPLES * SEQ, D), jnp.float32), jnp.arange(N_TP, dtype=jnp.int32))
    return (xf + total.reshape(SAMPLES, SEQ, D)).astype(jnp.bfloat16)
```

```python
import functools

import jax
import jax.numpy as jnp
from jax import lax
from jax.experimental import pallas as pl
from jax.experimental.pallas import tpu as pltpu
from jax.sharding import PartitionSpec as P

MESH = pl.DeviceIdType.MESH
F32, BF16 = jnp.float32, jnp.bfloat16
RIGHT, LEFT = 0, 1


def rem(a, b):
    return lax.rem(a, jnp.int32(b))


def div(a, b):
    return lax.div(a, jnp.int32(b))


def remote(src, dst, send_sem, recv_sem, device):
    return pltpu.make_async_remote_copy(
        src_ref=src, dst_ref=dst, send_sem=send_sem, recv_sem=recv_sem,
        device_id=device, device_id_type=MESH,
    )


def kernel(
    side, hid_hbm, w_hbm, ow_hbm, gain_ref, taps_ref, res_ref, rates_ref, skip_ref, len_ref, out_ref,
    hraw, hs, pbuf, ssq, acc, ext, qbuf, ubuf, cbuf, gated, st0, st1, st2, rs_out, rs_in,
    load_sem, ag_send, ag_recv, sib_send, sib_recv, rim_send, rim_recv,
    st0_send, st0_recv, st1_send, st1_recv, st2_send, st2_recv, rs_send, rs_recv,
):
    n = side * side
    half = n // 2
    samples, block, width = hid_hbm.shape
    rows = pbuf.shape[1]
    modes = rates_ref.shape[0]
    features = n * width
    me = lax.axis_index("ctx")
    z = lax.axis_index("tp")
    core = rem(me, 2)
    chip = div(me, 2)
    y, x = div(chip, side), rem(chip, side)
    turn = rem(x + y, side)
    sibling = {"ctx": me + 1 - 2 * core}

    def at(yy, xx):
        return {"ctx": 2 * (side * yy + xx) + core}

    def chip_first(q):
        a = div(q, side)
        return side * a + rem(q - side * a + side - a, side)

    def chip_second(q):
        a = div(q, side)
        return side * rem(q - side * a + side - a, side) + a

    def from_last(steps):
        return rem(me + 2 * n - steps, 2 * n)

    quarter = rows // 4
    rings = [
        (z, lambda q: {"tp": q}, lambda q, c: hraw.at[q, c]),
        (
            side * y + turn,
            lambda q: {"ctx": 2 * chip_first(q) + core},
            lambda q, c: pbuf.at[2 * chip_first(q) + core, pl.ds(quarter * c, quarter)],
        ),
        (
            side * x + turn,
            lambda q: {"ctx": 2 * chip_second(q) + core},
            lambda q, c: pbuf.at[2 * chip_second(q) + core, pl.ds(2 * quarter + quarter * c, quarter)],
        ),
    ]
    cycle_chip = [None, chip_first, chip_second]

    def owner(r, way, s):
        place = rings[r][0]
        return rem(place + n - s, n) if way == RIGHT else rem(place + s, n)

    def ag_start(r, way, s, c):
        place, device, view = rings[r]
        to = rem(place + 1, n) if way == RIGHT else rem(place + n - 1, n)
        block_ref = view(owner(r, way, s - 1), c)
        remote(block_ref, block_ref, ag_send.at[r, way, s - 1, c], ag_recv.at[r, way, s - 1, c], device(to)).start()

    def ag_arrived(r, way, s, c):
        place, device, view = rings[r]
        block_ref = view(owner(r, way, s), c)
        remote(block_ref, block_ref, ag_send.at[r, way, s - 1, c], ag_recv.at[r, way, s - 1, c], device(place)).wait_recv()

    def sib_view(r, way, s, which):
        return pbuf.at[
            2 * cycle_chip[r](owner(r, way, s)) + which, pl.ds(2 * quarter * (r - 1), 2 * quarter)
        ]

    def sib_start(r, way, s):
        part = sib_view(r, way, s, core)
        remote(part, part, sib_send.at[r - 1, way, s], sib_recv.at[r - 1, way, s], sibling).start()

    def sib_wait(r, way, s):
        part = sib_view(r, way, s, 1 - core)
        copy = remote(part, part, sib_send.at[r - 1, way, s], sib_recv.at[r - 1, way, s], sibling)
        copy.wait_send()
        copy.wait_recv()

    loads = [pltpu.make_async_copy(hid_hbm, hraw.at[z], load_sem.at[0])]
    for j in range(3):
        loads.append(pltpu.make_async_copy(
            w_hbm.at[j], pbuf.at[me, :, pl.ds(width * j, width)], load_sem.at[1 + j]))
    for j in range(2):
        loads.append(pltpu.make_async_copy(
            ow_hbm.at[pl.ds(rows * j, rows)], pbuf.at[me, :, pl.ds(3 * width + rows * j, rows)], load_sem.at[4 + j]))
    for copy in loads:
        copy.start()
    partners = [{"tp": rem(z + 1, n)}, {"tp": rem(z + n - 1, n)}, sibling, {"ctx": from_last(1)}]
    for j in range(1, side):
        partners.append(at(y, rem(x + j, side)))
        partners.append(at(rem(y + j, side), x))
    barrier = pltpu.get_barrier_semaphore()
    for partner in partners:
        pl.semaphore_signal(barrier, inc=1, device_id=partner, device_id_type=MESH)
    for copy in loads:
        copy.wait()
    pl.semaphore_wait(barrier, len(partners))

    def take(q):
        gain = gain_ref[pl.ds(q, 1), :]
        for s in range(samples):
            value = hraw[q, s].astype(F32)
            span = pl.ds(s * block, block)
            square = value * value
            ssq[span, :] = ssq[span, :] + square[:, : width // 2] + square[:, width // 2 :]
            hs[span, pl.ds(pl.multiple_of(q * width, width), width)] = (value * gain).astype(BF16)

    chunks = [(r, way, c) for c in range(2) for r in range(3) for way in (RIGHT, LEFT)]
    for r, way, c in chunks:
        ag_start(r, way, 1, c)
    for r in (1, 2):
        sib_start(r, RIGHT, 0)
    ssq[...] = jnp.zeros_like(ssq)
    take(z)

    def ag_step(s, carry):
        for r, way, c in chunks:
            ag_arrived(r, way, s, c)
            ag_start(r, way, s + 1, c)
        for r in (1, 2):
            for way in (RIGHT, LEFT):
                sib_start(r, way, s)
        take(owner(0, RIGHT, s))
        take(owner(0, LEFT, s))
        return carry

    lax.fori_loop(1, half - 1, ag_step, 0)
    for r, way, c in chunks:
        ag_arrived(r, way, half - 1, c)
        if c == way:
            ag_start(r, way, half, c)
    for r in (1, 2):
        for way in (RIGHT, LEFT):
            sib_start(r, way, half - 1)
    take(owner(0, RIGHT, half - 1))
    take(owner(0, LEFT, half - 1))
    for r in (1, 2, 0):
        for way in (RIGHT, LEFT):
            ag_arrived(r, way, half, way)
        if r:
            sib_start(r, RIGHT, half)
    take(owner(0, RIGHT, half))
    for r in (1, 2):
        sib_wait(r, RIGHT, 0)
        sib_wait(r, RIGHT, half)

    def sib_step(s, carry):
        for r in (1, 2):
            for way in (RIGHT, LEFT):
                sib_wait(r, way, s)
        return carry

    lax.fori_loop(1, half, sib_step, 0)

    deep = 4 if n % 4 == 0 else 1
    span_k = deep * width

    def product(i):
        left = hs[:, pl.ds(pl.multiple_of(i * span_k, span_k), span_k)]
        per = span_k // rows
        right = pbuf[pl.ds(i * per, per), :, : 3 * width].reshape(span_k, 3 * width)
        return jnp.dot(left, right, preferred_element_type=F32)

    acc[...] = product(jnp.int32(0))

    def project(i, carry):
        acc[...] = acc[...] + product(i)
        return carry

    lax.fori_loop(1, n // deep, project, 0)
    mean = jnp.sum(ssq[...], axis=1, keepdims=True) * (1.0 / features)
    scale = lax.rsqrt(mean + 1e-6)
    for s in range(samples):
        ext[s, 8:, :] = acc[s * block : (s + 1) * block, :] * scale[s * block : (s + 1) * block, :]
    rim = remote(ext.at[:, pl.ds(block, 8)], ext.at[:, pl.ds(0, 8)], rim_send, rim_recv, {"ctx": rem(me + 1, 2 * n)})
    rim.start()

    rates = rates_ref[...]
    decay = jnp.exp(-rates)
    whole = jnp.exp(-rates * float(block))
    coef = res_ref[...] * jnp.sqrt(2.0 * rates / modes)

    def powers(place, blocks):
        before, total = [], []
        for i in range(side):
            gap = jnp.maximum(place - 1 - i, 0).astype(F32)
            factor = jnp.exp(-rates * (gap * float(blocks * block)))
            before.append(jnp.where(i < place, factor, 0.0))
            total.append(jnp.exp(-rates * float(blocks * block * (side - 1 - i))))
        return before, total

    x_before, x_total = powers(x, 2)
    y_before, _ = powers(y, 2 * side)
    x_power = jnp.exp(-rates * (x.astype(F32) * float(2 * block)))

    rim.wait_recv()
    for s in range(samples):
        ext[s, :8, :] = jnp.where(me == 0, 0.0, ext[s, :8, :])

    def filtered(s, j):
        total = None
        for i in range(3):
            term = taps_ref[3 * i + j : 3 * i + j + 1, :] * ext[s, 8 - i : 8 - i + block, j * width : (j + 1) * width]
            total = term if total is None else total + term
        return total

    for s in range(samples):
        place = lax.broadcasted_iota(jnp.int32, (block, 1), 0) + me * block
        valid = jnp.where(place < len_ref[s], 1.0, 0.0)
        ubuf[s] = (filtered(s, 1) * filtered(s, 2) * valid).astype(BF16).astype(F32)
        qbuf[s] = filtered(s, 0) * valid

    def gather_state(g, states):
        states = list(states)
        tiles = [ubuf[s, pl.ds(pl.multiple_of(8 * g, 8), 8), :] for s in range(samples)]
        for i in range(8):
            for s in range(samples):
                states[s] = decay * states[s] + tiles[s][i : i + 1, :]
        return tuple(states)

    zero = jnp.zeros((modes, width), F32)
    ends = lax.fori_loop(0, block // 8, gather_state, (zero,) * samples)
    for s in range(samples):
        st0[core, s] = ends[s]
    pair = remote(st0.at[core], st0.at[core], st0_send, st0_recv, sibling)
    pair.start()
    pair_in = remote(st0.at[1 - core], st0.at[1 - core], st0_send, st0_recv, sibling)
    pair_in.wait_recv()
    for s in range(samples):
        st1[x, s] = whole * st0[0, s] + st0[1, s]
    for j in range(1, side):
        remote(st1.at[x], st1.at[x], st1_send.at[j], st1_recv.at[j], at(y, rem(x + j, side))).start()
    for j in range(1, side):
        slot = st1.at[rem(x + side - j, side)]
        remote(slot, slot, st1_send.at[j], st1_recv.at[j], sibling).wait_recv()
    for s in range(samples):
        st2[y, s] = sum(x_total[i] * st1[i, s] for i in range(side))
    for j in range(1, side):
        remote(st2.at[y], st2.at[y], st2_send.at[j], st2_recv.at[j], at(rem(y + j, side), x)).start()
    for j in range(1, side):
        slot = st2.at[rem(y + side - j, side)]
        remote(slot, slot, st2_send.at[j], st2_recv.at[j], sibling).wait_recv()
    incoming = []
    for s in range(samples):
        row = sum(y_before[i] * st2[i, s] for i in range(side))
        at_chip = x_power * row + sum(x_before[i] * st1[i, s] for i in range(side))
        incoming.append(jnp.where(core == 0, at_chip, whole * at_chip + st0[0, s]))

    def convolve(g, states):
        states = list(states)
        span = pl.ds(pl.multiple_of(8 * g, 8), 8)
        for s in range(samples):
            tile = ubuf[s, span, :]
            lines = []
            for i in range(8):
                states[s] = decay * states[s] + tile[i : i + 1, :]
                lines.append(jnp.sum(coef * states[s], axis=0, keepdims=True))
            cbuf[s, span, :] = jnp.concatenate(lines, axis=0)
        return tuple(states)

    lax.fori_loop(0, block // 8, convolve, tuple(incoming))
    for s in range(samples):
        gated[s] = (qbuf[s] * (cbuf[s] + skip_ref[...] * ubuf[s])).astype(BF16)

    def share(d, c):
        first, second = pbuf[2 * d, :, 3 * width :], pbuf[2 * d + 1, :, 3 * width :]
        right = jnp.concatenate([
            jnp.concatenate([first[:, :rows], second[:, :rows]], axis=1),
            jnp.concatenate([first[:, rows:], second[:, rows:]], axis=1),
        ], axis=0)
        return jnp.dot(gated[c], right, preferred_element_type=F32)

    def rs_copy(way, s, c):
        to = rem(z + 1, n) if way == RIGHT else rem(z + n - 1, n)
        return remote(
            rs_out.at[way, s - 1, c], rs_in.at[way, s - 1, c],
            rs_send.at[way, s - 1, c], rs_recv.at[way, s - 1, c], {"tp": to},
        )

    def rs_step(s, way, c, first):
        ahead = half + 1 - s
        d = rem(z + ahead, n) if way == RIGHT else rem(z + n - ahead, n)
        part = share(d, c)
        if not first:
            rs_copy(way, s - 1, c).wait_recv()
            part = part + rs_in[way, s - 2, c].astype(F32)
        rs_out[way, s - 1, c] = part.astype(BF16)
        rs_copy(way, s, c).start()

    for c in range(2):
        rs_step(1, c, c, True)
    for way, c in ((RIGHT, 1), (LEFT, 0), (RIGHT, 0), (LEFT, 1)):
        rs_step(2, way, c, way != c)

    def reduce_step(s, carry):
        for way, c in ((RIGHT, 1), (LEFT, 0), (RIGHT, 0), (LEFT, 1)):
            rs_step(s, way, c, False)
        return carry

    lax.fori_loop(3, half + 1, reduce_step, 0)
    for c in range(samples):
        part = share(z, c) + hraw[z, c].astype(F32)
        for way in (RIGHT, LEFT):
            rs_copy(way, half, c).wait_recv()
            part = part + rs_in[way, half - 1, c].astype(F32)
        out_ref[c] = part.astype(BF16)

    def ag_sent(r, way, s, c):
        place, device, view = rings[r]
        block_ref = view(owner(r, way, s - 1), c)
        remote(block_ref, block_ref, ag_send.at[r, way, s - 1, c], ag_recv.at[r, way, s - 1, c], device(place)).wait_send()

    def sent(s, carry):
        for r, way, c in chunks:
            ag_sent(r, way, s, c)
        return carry

    lax.fori_loop(1, half, sent, 0)
    for r in range(3):
        for way in (RIGHT, LEFT):
            ag_sent(r, way, half, way)
    rim.wait_send()
    pair.wait_send()
    for j in range(1, side):
        remote(st1.at[x], st1.at[x], st1_send.at[j], st1_recv.at[j], sibling).wait_send()
        remote(st2.at[y], st2.at[y], st2_send.at[j], st2_recv.at[j], sibling).wait_send()
    for c in range(2):
        rs_copy(c, 1, c).wait_send()

    def reduced(s, carry):
        for way in (RIGHT, LEFT):
            for c in range(2):
                rs_copy(way, s, c).wait_send()
        return carry

    lax.fori_loop(2, half + 1, reduced, 0)


def on_device(hidden, norm_gain, in_weight, short_weight, residues, rates, skip_gain, out_weight, lengths):
    samples, block, width = hidden.shape
    rows = in_weight.shape[0]
    n = lax.axis_size("tp")
    side = int(round(n ** 0.5))
    half = n // 2
    modes = rates.shape[0]
    dma = pltpu.SemaphoreType.DMA
    hbm = pl.BlockSpec(memory_space=pl.ANY)
    vmem = pl.BlockSpec(memory_space=pltpu.VMEM)
    state = (samples, modes, width)
    return pl.pallas_call(
        functools.partial(kernel, side),
        out_shape=jax.ShapeDtypeStruct(hidden.shape, BF16),
        in_specs=[hbm, hbm, hbm] + [vmem] * 5 + [pl.BlockSpec(memory_space=pltpu.SMEM)],
        out_specs=vmem,
        scratch_shapes=[
            pltpu.VMEM((n, samples, block, width), BF16),
            pltpu.VMEM((samples * block, n * width), BF16),
            pltpu.VMEM((2 * n, rows, 3 * width + 2 * rows), BF16),
            pltpu.VMEM((samples * block, width // 2), F32),
            pltpu.VMEM((samples * block, 3 * width), F32),
            pltpu.VMEM((samples, block + 8, 3 * width), F32),
            pltpu.VMEM((samples, block, width), F32),
            pltpu.VMEM((samples, block, width), F32),
            pltpu.VMEM((samples, block, width), F32),
            pltpu.VMEM((samples, block, width), BF16),
            pltpu.VMEM((2,) + state, F32),
            pltpu.VMEM((side,) + state, F32),
            pltpu.VMEM((side,) + state, F32),
            pltpu.VMEM((2, half, 2, block, width), BF16),
            pltpu.VMEM((2, half, 2, block, width), BF16),
            dma((6,)),
            dma((3, 2, half, 2)),
            dma((3, 2, half, 2)),
            dma((2, 2, half + 1)),
            dma((2, 2, half + 1)),
            dma,
            dma,
            dma,
            dma,
            dma((side,)),
            dma((side,)),
            dma((side,)),
            dma((side,)),
            dma((2, half, 2)),
            dma((2, half, 2)),
        ],
        compiler_params=pltpu.CompilerParams(
            collective_id=0, has_side_effects=True, vmem_limit_bytes=48 * 2**20
        ),
    )(
        hidden,
        jnp.transpose(in_weight, (1, 0, 2)),
        out_weight,
        norm_gain.reshape(n, width),
        short_weight.reshape(-1, width),
        residues,
        rates,
        skip_gain.reshape(1, width),
        lengths,
    )


def solution(mesh):
    placed = (
        P(None, "ctx", "tp"),
        P(),
        P("ctx", None, "tp"),
        P(None, None, "tp"),
        P(None, "tp"),
        P(None, "tp"),
        P("tp"),
        P("tp", "ctx"),
        P(),
    )
    return jax.shard_map(
        on_device, mesh=mesh, in_specs=placed, out_specs=P(None, "ctx", "tp"), check_vma=False
    )
```

```python
import functools

import jax
import jax.numpy as jnp
from jax import lax
from jax.experimental import pallas as pl
from jax.experimental.pallas import tpu as pltpu
from jax.sharding import PartitionSpec as P

MESH = pl.DeviceIdType.MESH
F32, BF16 = jnp.float32, jnp.bfloat16
RIGHT, LEFT = 0, 1
CHUNKS = 4


def rem(a, b):
    return lax.rem(a, jnp.int32(b))


def div(a, b):
    return lax.div(a, jnp.int32(b))


def remote(src, dst, send_sem, recv_sem, device):
    return pltpu.make_async_remote_copy(
        src_ref=src, dst_ref=dst, send_sem=send_sem, recv_sem=recv_sem,
        device_id=device, device_id_type=MESH,
    )


def kernel(
    side, hid_hbm, w_hbm, ow_hbm, gain_hbm, taps_hbm, res_hbm, rates_hbm, skip_hbm, len_ref, out_ref,
    gain_ref, taps_ref, res_ref, rates_ref, skip_ref,
    hraw, hs, pbuf, ssq, acc, ext, qbuf, ubuf, cbuf, gated, table, st_in, st0, st1, st2, parts, rs_out, rs_in,
    load_sem, ag_send, ag_recv, sib_send, sib_recv, rim_send, rim_recv,
    st0_send, st0_recv, st1_send, st1_recv, st2_send, st2_recv, rs_send, rs_recv,
):
    n = side * side
    half = n // 2
    samples, block, width = ubuf.shape
    rows = pbuf.shape[1]
    piece = samples * block // CHUNKS
    modes = rates_ref.shape[0]
    features = n * width
    me = lax.axis_index("ctx")
    z = lax.axis_index("tp")
    core = rem(me, 2)
    chip = div(me, 2)
    y, x = div(chip, side), rem(chip, side)
    turn = rem(x + y, side)
    sibling = {"ctx": me + 1 - 2 * core}

    def at(yy, xx):
        return {"ctx": 2 * (side * yy + xx) + core}

    def chip_first(q):
        a = div(q, side)
        return side * a + rem(q - side * a + side - a, side)

    def chip_second(q):
        a = div(q, side)
        return side * rem(q - side * a + side - a, side) + a

    def from_last(steps):
        return rem(me + 2 * n - steps, 2 * n)

    quarter = rows // (2 * CHUNKS)
    first_place, second_place = side * y + turn, side * x + turn

    def ring(place, slot, device, chunk):
        return place, slot, chunk, (device(rem(place + 1, n)), device(rem(place + n - 1, n)))

    def first_slot(q):
        return 2 * chip_first(q) + core

    def second_slot(q):
        return 2 * chip_second(q) + core

    rings = [
        ring(z, lambda q: q, lambda q: {"tp": q}, lambda at_slot, c: hraw.at[at_slot, pl.ds(piece * c, piece)]),
        ring(
            first_place, first_slot, lambda q: {"ctx": first_slot(q)},
            lambda at_slot, c: pbuf.at[at_slot, pl.ds(quarter * c, quarter)],
        ),
        ring(
            second_place, second_slot, lambda q: {"ctx": second_slot(q)},
            lambda at_slot, c: pbuf.at[at_slot, pl.ds(rows // 2 + quarter * c, quarter)],
        ),
    ]

    def slot_of(r, way, s):
        place, slot = rings[r][:2]
        return slot(rem(place + n - s, n) if way == RIGHT else rem(place + s, n))

    def ag_copy(r, way, s, c, at_slot):
        part = rings[r][2](at_slot, c)
        return remote(part, part, ag_send.at[r, way, s - 1, c], ag_recv.at[r, way, s - 1, c], rings[r][3][way])

    def ag_start(r, way, s, c, at_slot):
        ag_copy(r, way, s, c, at_slot).start()

    def ag_arrived(r, way, s, c):
        ag_copy(r, way, s, c, 0).wait_recv()

    def ag_sent(r, way, s, c):
        ag_copy(r, way, s, c, 0).wait_send()

    def sib_copy(r, way, s, at_slot):
        part = pbuf.at[at_slot, pl.ds(rows // 2 * (r - 1), rows // 2)]
        return remote(part, part, sib_send.at[r - 1, way, s], sib_recv.at[r - 1, way, s], sibling)

    def sib_wait(r, way, s):
        copy = sib_copy(r, way, s, 0)
        copy.wait_send()
        copy.wait_recv()

    loads = [pltpu.make_async_copy(hid_hbm, hraw.at[z], load_sem.at[0])]
    for j in range(3):
        loads.append(pltpu.make_async_copy(
            w_hbm.at[j], pbuf.at[me, :, pl.ds(width * j, width)], load_sem.at[1 + j]))
    for j in range(2):
        loads.append(pltpu.make_async_copy(
            ow_hbm.at[pl.ds(rows * j, rows)], pbuf.at[me, :, pl.ds(3 * width + rows * j, rows)], load_sem.at[4 + j]))
    small = [(gain_hbm, gain_ref), (taps_hbm, taps_ref), (res_hbm, res_ref), (rates_hbm, rates_ref), (skip_hbm, skip_ref)]
    for j, (source, target) in enumerate(small):
        loads.append(pltpu.make_async_copy(source, target, load_sem.at[6 + j]))
    for copy in loads:
        copy.start()
    partners = [{"tp": rem(z + 1, n)}, {"tp": rem(z + n - 1, n)}, sibling, {"ctx": from_last(1)}]
    for j in range(1, side):
        partners.append(at(y, rem(x + j, side)))
        partners.append(at(rem(y + j, side), x))
    barrier = pltpu.get_barrier_semaphore()
    for partner in partners:
        pl.semaphore_signal(barrier, inc=1, device_id=partner, device_id_type=MESH)
    for copy in loads:
        copy.wait()
    pl.semaphore_wait(barrier, len(partners))

    def take(q):
        gain = gain_ref[:, pl.ds(pl.multiple_of(q * width, width), width)]
        for s in range(samples):
            value = hraw[q, s * block : (s + 1) * block, :].astype(F32)
            span = pl.ds(s * block, block)
            square = value * value
            ssq[span, :] = ssq[span, :] + square[:, : width // 2] + square[:, width // 2 :]
            hs[span, pl.ds(pl.multiple_of(q * width, width), width)] = (value * gain).astype(BF16)

    def goes_far(way, c):
        return (c < CHUNKS // 2) == (way == RIGHT)

    lanes = [(r, way) for r in range(3) for way in (RIGHT, LEFT)]
    mine = [z, me, me]
    for c in range(CHUNKS):
        for r, way in lanes:
            ag_start(r, way, 1, c, mine[r])
    for r in (1, 2):
        sib_copy(r, RIGHT, 0, me).start()
    ssq[...] = jnp.zeros_like(ssq)
    take(z)

    def ag_step(s, carry):
        slots = {(r, way): slot_of(r, way, s) for r, way in lanes}
        for c in range(CHUNKS):
            for r, way in lanes:
                ag_arrived(r, way, s, c)
                ag_start(r, way, s + 1, c, slots[r, way])
        for r, way in lanes[2:]:
            sib_copy(r, way, s, slots[r, way]).start()
        take(slots[0, RIGHT])
        take(slots[0, LEFT])
        return carry

    lax.fori_loop(1, half - 1, ag_step, 0)
    slots = {(r, way): slot_of(r, way, half - 1) for r, way in lanes}
    for c in range(CHUNKS):
        for r, way in lanes:
            ag_arrived(r, way, half - 1, c)
            if goes_far(way, c):
                ag_start(r, way, half, c, slots[r, way])
    for r, way in lanes[2:]:
        sib_copy(r, way, half - 1, slots[r, way]).start()
    take(slots[0, RIGHT])
    take(slots[0, LEFT])
    for r in (1, 2, 0):
        for c in range(CHUNKS):
            ag_arrived(r, RIGHT if goes_far(RIGHT, c) else LEFT, half, c)
        if r:
            sib_copy(r, RIGHT, half, slot_of(r, RIGHT, half)).start()
    take(slot_of(0, RIGHT, half))
    for r in (1, 2):
        sib_wait(r, RIGHT, 0)
        sib_wait(r, RIGHT, half)

    def sib_step(s, carry):
        for r in (1, 2):
            for way in (RIGHT, LEFT):
                sib_wait(r, way, s)
        return carry

    lax.fori_loop(1, half, sib_step, 0)

    deep = 4 if n % 4 == 0 else 1
    span_k = deep * width

    def product(i):
        left = hs[:, pl.ds(pl.multiple_of(i * span_k, span_k), span_k)]
        per = span_k // rows
        right = pbuf[pl.ds(i * per, per), :, : 3 * width].reshape(span_k, 3 * width)
        return jnp.dot(left, right, preferred_element_type=F32)

    acc[...] = product(jnp.int32(0))

    def project(i, carry):
        acc[...] = acc[...] + product(i)
        return carry

    lax.fori_loop(1, n // deep, project, 0)
    mean = jnp.sum(ssq[...], axis=1, keepdims=True) * (1.0 / features)
    scale = lax.rsqrt(mean + 1e-6)
    for s in range(samples):
        ext[s, 8:, :] = acc[s * block : (s + 1) * block, :] * scale[s * block : (s + 1) * block, :]
    rim = remote(ext.at[:, pl.ds(block, 8)], ext.at[:, pl.ds(0, 8)], rim_send, rim_recv, {"ctx": rem(me + 1, 2 * n)})
    rim.start()

    rates = rates_ref[...]
    decay = jnp.exp(-rates)
    whole = jnp.exp(-rates * float(block))
    coef = res_ref[...] * jnp.sqrt(2.0 * rates / modes)

    def powers(place, blocks):
        before, total = [], []
        for i in range(side):
            gap = jnp.maximum(place - 1 - i, 0).astype(F32)
            factor = jnp.exp(-rates * (gap * float(blocks * block)))
            before.append(jnp.where(i < place, factor, 0.0))
            total.append(jnp.exp(-rates * float(blocks * block * (side - 1 - i))))
        return before, total

    def filtered(s, j, first, count):
        total = None
        for i in range(3):
            term = taps_ref[i, j : j + 1, :] * ext[s, 8 + first - i : 8 + first - i + count, j * width : (j + 1) * width]
            total = term if total is None else total + term
        return total

    def features_of(first, count):
        for s in range(samples):
            place = lax.broadcasted_iota(jnp.int32, (count, 1), 0) + (me * block + first)
            valid = jnp.where(place < len_ref[s], 1.0, 0.0)
            span = slice(first, first + count)
            pushed = filtered(s, 1, first, count) * filtered(s, 2, first, count) * valid
            ubuf[s, span, :] = pushed.astype(BF16).astype(F32)
            qbuf[s, span, :] = filtered(s, 0, first, count) * valid

    def gather_state(g, states):
        states = list(states)
        tiles = [ubuf[s, pl.ds(pl.multiple_of(8 * g, 8), 8), :] for s in range(samples)]
        for i in range(8):
            for s in range(samples):
                states[s] = decay * states[s] + tiles[s][i : i + 1, :]
        return tuple(states)

    zero = jnp.zeros((modes, width), F32)
    features_of(8, block - 8)
    ends = lax.fori_loop(1, block // 8, gather_state, (zero,) * samples)
    rim.wait_recv()
    for s in range(samples):
        ext[s, :8, :] = jnp.where(me == 0, 0.0, ext[s, :8, :])
    features_of(0, 8)
    heads = gather_state(0, (zero,) * samples)
    late = jnp.exp(-rates * float(block - 8))
    for s in range(samples):
        st0[core, s] = late * heads[s] + ends[s]
    pair = remote(st0.at[core], st0.at[core], st0_send, st0_recv, sibling)
    pair.start()

    def fill_table(m, carry):
        rate = rates_ref[pl.ds(m, 1), :]
        steps = lax.broadcasted_iota(jnp.int32, (block, 1), 0).astype(F32) + 1.0
        table[m] = res_ref[pl.ds(m, 1), :] * jnp.sqrt(2.0 * rate / modes) * jnp.exp(-rate * steps)
        return carry

    def convolve(s):
        def body(g, state):
            span = pl.ds(pl.multiple_of(8 * g, 8), 8)
            tile = ubuf[s, span, :]
            lines = []
            for i in range(8):
                state = decay * state + tile[i : i + 1, :]
                lines.append(jnp.sum(coef * state, axis=0, keepdims=True))
            cbuf[s, span, :] = jnp.concatenate(lines, axis=0)
            return state

        lax.fori_loop(0, block // 8, body, zero)

    x_before, x_total = powers(x, 2)
    lax.fori_loop(0, modes, fill_table, 0)
    pair_in = remote(st0.at[1 - core], st0.at[1 - core], st0_send, st0_recv, sibling)
    pair_in.wait_recv()
    for s in range(samples):
        st1[x, s] = whole * st0[0, s] + st0[1, s]
    for j in range(1, side):
        remote(st1.at[x], st1.at[x], st1_send.at[j], st1_recv.at[j], at(y, rem(x + j, side))).start()
    y_before, _ = powers(y, 2 * side)
    x_power = jnp.exp(-rates * (x.astype(F32) * float(2 * block)))
    convolve(0)
    for j in range(1, side):
        slot = st1.at[rem(x + side - j, side)]
        remote(slot, slot, st1_send.at[j], st1_recv.at[j], sibling).wait_recv()
    for s in range(samples):
        st2[y, s] = sum(x_total[i] * st1[i, s] for i in range(side))
    for j in range(1, side):
        remote(st2.at[y], st2.at[y], st2_send.at[j], st2_recv.at[j], at(rem(y + j, side), x)).start()
    convolve(1)
    for j in range(1, side):
        slot = st2.at[rem(y + side - j, side)]
        remote(slot, slot, st2_send.at[j], st2_recv.at[j], sibling).wait_recv()
    for s in range(samples):
        row = sum(y_before[i] * st2[i, s] for i in range(side))
        at_chip = x_power * row + sum(x_before[i] * st1[i, s] for i in range(side))
        st_in[s] = jnp.where(core == 0, at_chip, whole * at_chip + st0[0, s])

    tall = 32

    def carry_in(g, carry):
        span = pl.ds(pl.multiple_of(tall * g, tall), tall)
        totals = [cbuf[s, span, :] + skip_ref[...] * ubuf[s, span, :] for s in range(samples)]
        for m in range(modes):
            weight = table[m, span, :]
            for s in range(samples):
                totals[s] = totals[s] + weight * st_in[s, m : m + 1, :]
        for s in range(samples):
            target = pl.ds(pl.multiple_of(block * s + tall * g, tall), tall)
            gated[target, :] = (qbuf[s, span, :] * totals[s]).astype(BF16)
        return carry

    lax.fori_loop(0, block // tall, carry_in, 0)

    def share(d):
        first, second = pbuf[2 * d, :, 3 * width :], pbuf[2 * d + 1, :, 3 * width :]
        right = jnp.concatenate([
            jnp.concatenate([first[:, :rows], second[:, :rows]], axis=1),
            jnp.concatenate([first[:, rows:], second[:, rows:]], axis=1),
        ], axis=0)
        return jnp.dot(gated[...], right, preferred_element_type=F32)

    def rs_copy(way, s, c):
        return remote(
            rs_out.at[way, s - 1, c], rs_in.at[way, s - 1, c],
            rs_send.at[way, s - 1, c], rs_recv.at[way, s - 1, c], rings[0][3][way],
        )

    def prepare(s):
        ahead = half + 1 - s
        parts[RIGHT] = share(rem(z + ahead, n))
        parts[LEFT] = share(rem(z + n - ahead, n))

    def rs_step(s, way, c, first):
        part = parts[way, piece * c : piece * (c + 1), :]
        if not first:
            rs_copy(way, s - 1, c).wait_recv()
            part = part + rs_in[way, s - 2, c].astype(F32)
        rs_out[way, s - 1, c] = part.astype(BF16)
        rs_copy(way, s, c).start()

    order = [(way, c) for far in (False, True) for c in range(CHUNKS) for way in (RIGHT, LEFT) if goes_far(way, c) == far]
    farthest = share(rem(z + half, n))
    for c in range(CHUNKS):
        way = RIGHT if goes_far(RIGHT, c) else LEFT
        rs_out[way, 0, c] = farthest[piece * c : piece * (c + 1), :].astype(BF16)
        rs_copy(way, 1, c).start()
    prepare(2)
    for way, c in order:
        rs_step(2, way, c, not goes_far(way, c))

    def reduce_step(s, carry):
        prepare(s)
        for way, c in order:
            rs_step(s, way, c, False)
        return carry

    lax.fori_loop(3, half + 1, reduce_step, 0)
    own = share(z)
    for c in range(CHUNKS):
        span = slice(piece * c, piece * (c + 1))
        part = own[span, :] + hraw[z, span, :].astype(F32)
        for way in (RIGHT, LEFT):
            rs_copy(way, half, c).wait_recv()
            part = part + rs_in[way, half - 1, c].astype(F32)
        out_ref[span, :] = part.astype(BF16)

    def sent(s, carry):
        for r, way in lanes:
            for c in range(CHUNKS):
                ag_sent(r, way, s, c)
        return carry

    lax.fori_loop(1, half, sent, 0)
    for r, way in lanes:
        for c in range(CHUNKS):
            if goes_far(way, c):
                ag_sent(r, way, half, c)
    rim.wait_send()
    pair.wait_send()
    for j in range(1, side):
        remote(st1.at[x], st1.at[x], st1_send.at[j], st1_recv.at[j], sibling).wait_send()
        remote(st2.at[y], st2.at[y], st2_send.at[j], st2_recv.at[j], sibling).wait_send()

    def reduced(s, carry):
        for way in (RIGHT, LEFT):
            for c in range(CHUNKS):
                rs_copy(way, s, c).wait_send()
        return carry

    lax.fori_loop(2, half + 1, reduced, 0)
    for c in range(CHUNKS):
        rs_copy(RIGHT if goes_far(RIGHT, c) else LEFT, 1, c).wait_send()


def on_device(hidden, norm_gain, in_weight, short_weight, residues, rates, skip_gain, out_weight, lengths):
    samples, block, width = hidden.shape
    rows = in_weight.shape[0]
    n = lax.axis_size("tp")
    side = int(round(n ** 0.5))
    half = n // 2
    modes = rates.shape[0]
    dma = pltpu.SemaphoreType.DMA
    hbm = pl.BlockSpec(memory_space=pltpu.HBM)
    vmem = pl.BlockSpec(memory_space=pltpu.VMEM)
    state = (samples, modes, width)
    return pl.pallas_call(
        functools.partial(kernel, side),
        out_shape=jax.ShapeDtypeStruct((samples * block, width), BF16),
        in_specs=[hbm] * 8 + [pl.BlockSpec(memory_space=pltpu.SMEM)],
        out_specs=vmem,
        scratch_shapes=[
            pltpu.VMEM((1, n * width), F32),
            pltpu.VMEM(short_weight.shape, F32),
            pltpu.VMEM(rates.shape, F32),
            pltpu.VMEM(rates.shape, F32),
            pltpu.VMEM((1, width), F32),
            pltpu.VMEM((n, samples * block, width), BF16),
            pltpu.VMEM((samples * block, n * width), BF16),
            pltpu.VMEM((2 * n, rows, 3 * width + 2 * rows), BF16),
            pltpu.VMEM((samples * block, width // 2), F32),
            pltpu.VMEM((samples * block, 3 * width), F32),
            pltpu.VMEM((samples, block + 8, 3 * width), F32),
            pltpu.VMEM((samples, block, width), F32),
            pltpu.VMEM((samples, block, width), F32),
            pltpu.VMEM((samples, block, width), F32),
            pltpu.VMEM((samples * block, width), BF16),
            pltpu.VMEM((modes, block, width), F32),
            pltpu.VMEM(state, F32),
            pltpu.VMEM((2,) + state, F32),
            pltpu.VMEM((side,) + state, F32),
            pltpu.VMEM((side,) + state, F32),
            pltpu.VMEM((2, samples * block, width), F32),
            pltpu.VMEM((2, half, CHUNKS, samples * block // CHUNKS, width), BF16),
            pltpu.VMEM((2, half, CHUNKS, samples * block // CHUNKS, width), BF16),
            dma((11,)),
            dma((3, 2, half, CHUNKS)),
            dma((3, 2, half, CHUNKS)),
            dma((2, 2, half + 1)),
            dma((2, 2, half + 1)),
            dma,
            dma,
            dma,
            dma,
            dma((side,)),
            dma((side,)),
            dma((side,)),
            dma((side,)),
            dma((2, half, CHUNKS)),
            dma((2, half, CHUNKS)),
        ],
        compiler_params=pltpu.CompilerParams(
            collective_id=0, has_side_effects=True, vmem_limit_bytes=60 * 2**20
        ),
    )(
        hidden.reshape(samples * block, width),
        jnp.transpose(in_weight, (1, 0, 2)),
        out_weight,
        norm_gain.reshape(1, n * width),
        short_weight,
        residues,
        rates,
        skip_gain.reshape(1, width),
        lengths,
    ).reshape(hidden.shape)


def solution(mesh):
    placed = (
        P(None, "ctx", "tp"),
        P(),
        P("ctx", None, "tp"),
        P(None, None, "tp"),
        P(None, "tp"),
        P(None, "tp"),
        P("tp"),
        P("tp", "ctx"),
        P(),
    )
    return jax.shard_map(
        on_device, mesh=mesh, in_specs=placed, out_specs=P(None, "ctx", "tp"), check_vma=False
    )
```

```python
import functools

import jax
import jax.numpy as jnp
from jax import lax
from jax.experimental import pallas as pl
from jax.experimental.pallas import tpu as pltpu
from jax.sharding import PartitionSpec as P

MESH = pl.DeviceIdType.MESH
F32, BF16 = jnp.float32, jnp.bfloat16
RIGHT, LEFT = 0, 1
CHUNKS = 4


def rem(a, b):
    return lax.rem(a, jnp.int32(b))


def div(a, b):
    return lax.div(a, jnp.int32(b))


def remote(src, dst, send_sem, recv_sem, device):
    return pltpu.make_async_remote_copy(
        src_ref=src, dst_ref=dst, send_sem=send_sem, recv_sem=recv_sem,
        device_id=device, device_id_type=MESH,
    )


def kernel(
    side, hid_hbm, w_hbm, ow_hbm, gain_hbm, taps_hbm, res_hbm, rates_hbm, skip_hbm, len_ref, out_ref,
    gain_ref, taps_ref, res_ref, rates_ref, skip_ref,
    hraw, hs, pbuf, ssq, acc, ext, qbuf, ubuf, cbuf, gated, table, st_in, st0, st1, st2, parts, own, rs_out, rs_in,
    load_sem, ag_send, ag_recv, sib_send, sib_recv, rim_send, rim_recv,
    st0_send, st0_recv, st1_send, st1_recv, st2_send, st2_recv, rs_send, rs_recv,
):
    n = side * side
    half = n // 2
    samples, block, width = ubuf.shape
    rows = pbuf.shape[1]
    piece = samples * block // CHUNKS
    modes = rates_ref.shape[0]
    features = n * width
    me = lax.axis_index("ctx")
    z = lax.axis_index("tp")
    core = rem(me, 2)
    chip = div(me, 2)
    y, x = div(chip, side), rem(chip, side)
    turn = rem(x + y, side)
    sibling = {"ctx": me + 1 - 2 * core}

    def at(yy, xx):
        return {"ctx": 2 * (side * yy + xx) + core}

    def chip_first(q):
        a = div(q, side)
        return side * a + rem(q - side * a + side - a, side)

    def chip_second(q):
        a = div(q, side)
        return side * rem(q - side * a + side - a, side) + a

    def from_last(steps):
        return rem(me + 2 * n - steps, 2 * n)

    quarter = rows // (2 * CHUNKS)
    first_place, second_place = side * y + turn, side * x + turn

    def ring(place, slot, device, chunk):
        return place, slot, chunk, (device(rem(place + 1, n)), device(rem(place + n - 1, n)))

    def first_slot(q):
        return 2 * chip_first(q) + core

    def second_slot(q):
        return 2 * chip_second(q) + core

    rings = [
        ring(z, lambda q: q, lambda q: {"tp": q}, lambda at_slot, c: hraw.at[at_slot, pl.ds(piece * c, piece)]),
        ring(
            first_place, first_slot, lambda q: {"ctx": first_slot(q)},
            lambda at_slot, c: pbuf.at[at_slot, pl.ds(quarter * c, quarter)],
        ),
        ring(
            second_place, second_slot, lambda q: {"ctx": second_slot(q)},
            lambda at_slot, c: pbuf.at[at_slot, pl.ds(rows // 2 + quarter * c, quarter)],
        ),
    ]

    def slot_of(r, way, s):
        place, slot = rings[r][:2]
        return slot(rem(place + n - s, n) if way == RIGHT else rem(place + s, n))

    def ag_copy(r, way, s, c, at_slot):
        part = rings[r][2](at_slot, c)
        return remote(part, part, ag_send.at[r, way, s - 1, c], ag_recv.at[r, way, s - 1, c], rings[r][3][way])

    def ag_start(r, way, s, c, at_slot):
        ag_copy(r, way, s, c, at_slot).start()

    def ag_arrived(r, way, s, c):
        ag_copy(r, way, s, c, 0).wait_recv()

    def ag_sent(r, way, s, c):
        ag_copy(r, way, s, c, 0).wait_send()

    def sib_copy(r, way, s, at_slot):
        part = pbuf.at[at_slot, pl.ds(rows // 2 * (r - 1), rows // 2)]
        return remote(part, part, sib_send.at[r - 1, way, s], sib_recv.at[r - 1, way, s], sibling)

    def sib_wait(r, way, s):
        copy = sib_copy(r, way, s, 0)
        copy.wait_send()
        copy.wait_recv()

    loads = [pltpu.make_async_copy(hid_hbm, hraw.at[z], load_sem.at[0])]
    for j in range(3):
        loads.append(pltpu.make_async_copy(
            w_hbm.at[j], pbuf.at[me, :, pl.ds(width * j, width)], load_sem.at[1 + j]))
    for j in range(2):
        loads.append(pltpu.make_async_copy(
            ow_hbm.at[pl.ds(rows * j, rows)], pbuf.at[me, :, pl.ds(3 * width + rows * j, rows)], load_sem.at[4 + j]))
    small = [(gain_hbm, gain_ref), (taps_hbm, taps_ref), (res_hbm, res_ref), (rates_hbm, rates_ref), (skip_hbm, skip_ref)]
    for j, (source, target) in enumerate(small):
        loads.append(pltpu.make_async_copy(source, target, load_sem.at[6 + j]))
    for copy in loads:
        copy.start()
    partners = [{"tp": rem(z + 1, n)}, {"tp": rem(z + n - 1, n)}, sibling, {"ctx": from_last(1)}]
    for j in range(1, side):
        partners.append(at(y, rem(x + j, side)))
        partners.append(at(rem(y + j, side), x))
    barrier = pltpu.get_barrier_semaphore()
    for partner in partners:
        pl.semaphore_signal(barrier, inc=1, device_id=partner, device_id_type=MESH)
    for copy in loads:
        copy.wait()
    pl.semaphore_wait(barrier, len(partners))

    def take(q):
        gain = gain_ref[:, pl.ds(pl.multiple_of(q * width, width), width)]
        for s in range(samples):
            value = hraw[q, s * block : (s + 1) * block, :].astype(F32)
            span = pl.ds(s * block, block)
            square = value * value
            ssq[span, :] = ssq[span, :] + square[:, : width // 2] + square[:, width // 2 :]
            hs[span, pl.ds(pl.multiple_of(q * width, width), width)] = (value * gain).astype(BF16)

    def goes_far(way, c):
        return (c < CHUNKS // 2) == (way == RIGHT)

    lanes = [(r, way) for r in range(3) for way in (RIGHT, LEFT)]
    mine = [z, me, me]
    chunks = [(0, way, c) for c in range(CHUNKS) for way in (RIGHT, LEFT)]
    chunks += [(r, way, c) for c in range(CHUNKS) for r, way in lanes[2:]]
    for r, way, c in chunks:
        ag_start(r, way, 1, c, mine[r])
    for r in (1, 2):
        sib_copy(r, RIGHT, 0, me).start()
    ssq[...] = jnp.zeros_like(ssq)
    take(z)

    def ag_step(s, carry):
        slots = {(r, way): slot_of(r, way, s) for r, way in lanes}
        for r, way, c in chunks:
            ag_arrived(r, way, s, c)
            ag_start(r, way, s + 1, c, slots[r, way])
        for r, way in lanes[2:]:
            sib_copy(r, way, s, slots[r, way]).start()
        take(slots[0, RIGHT])
        take(slots[0, LEFT])
        return carry

    lax.fori_loop(1, half - 1, ag_step, 0)
    slots = {(r, way): slot_of(r, way, half - 1) for r, way in lanes}
    for r, way, c in chunks:
        ag_arrived(r, way, half - 1, c)
        if goes_far(way, c):
            ag_start(r, way, half, c, slots[r, way])
    for r, way in lanes[2:]:
        sib_copy(r, way, half - 1, slots[r, way]).start()
    take(slots[0, RIGHT])
    take(slots[0, LEFT])
    for r in (1, 2, 0):
        for c in range(CHUNKS):
            ag_arrived(r, RIGHT if goes_far(RIGHT, c) else LEFT, half, c)
        if r:
            sib_copy(r, RIGHT, half, slot_of(r, RIGHT, half)).start()
    take(slot_of(0, RIGHT, half))
    for r in (1, 2):
        sib_wait(r, RIGHT, 0)
        sib_wait(r, RIGHT, half)

    def sib_step(s, carry):
        for r in (1, 2):
            for way in (RIGHT, LEFT):
                sib_wait(r, way, s)
        return carry

    lax.fori_loop(1, half, sib_step, 0)

    deep = 4 if n % 4 == 0 else 1
    span_k = deep * width

    def product(i):
        left = hs[:, pl.ds(pl.multiple_of(i * span_k, span_k), span_k)]
        per = span_k // rows
        right = pbuf[pl.ds(i * per, per), :, : 3 * width].reshape(span_k, 3 * width)
        return jnp.dot(left, right, preferred_element_type=F32)

    acc[...] = product(jnp.int32(0))

    def project(i, carry):
        acc[...] = acc[...] + product(i)
        return carry

    lax.fori_loop(1, n // deep, project, 0)
    mean = jnp.sum(ssq[...], axis=1, keepdims=True) * (1.0 / features)
    scale = lax.rsqrt(mean + 1e-6)
    for s in range(samples):
        ext[s, 8:, :] = acc[s * block : (s + 1) * block, :] * scale[s * block : (s + 1) * block, :]
    rim = remote(ext.at[:, pl.ds(block, 8)], ext.at[:, pl.ds(0, 8)], rim_send, rim_recv, {"ctx": rem(me + 1, 2 * n)})
    rim.start()

    rates = rates_ref[...]
    decay = jnp.exp(-rates)
    whole = jnp.exp(-rates * float(block))
    coef = res_ref[...] * jnp.sqrt(2.0 * rates / modes)

    def powers(place, blocks):
        before, total = [], []
        for i in range(side):
            gap = jnp.maximum(place - 1 - i, 0).astype(F32)
            factor = jnp.exp(-rates * (gap * float(blocks * block)))
            before.append(jnp.where(i < place, factor, 0.0))
            total.append(jnp.exp(-rates * float(blocks * block * (side - 1 - i))))
        return before, total

    def filtered(s, j, first, count):
        total = None
        for i in range(3):
            term = taps_ref[i, j : j + 1, :] * ext[s, 8 + first - i : 8 + first - i + count, j * width : (j + 1) * width]
            total = term if total is None else total + term
        return total

    def features_of(first, count):
        for s in range(samples):
            place = lax.broadcasted_iota(jnp.int32, (count, 1), 0) + (me * block + first)
            valid = jnp.where(place < len_ref[s], 1.0, 0.0)
            span = slice(first, first + count)
            pushed = filtered(s, 1, first, count) * filtered(s, 2, first, count) * valid
            ubuf[s, span, :] = pushed.astype(BF16).astype(F32)
            qbuf[s, span, :] = filtered(s, 0, first, count) * valid

    def gather_state(g, states):
        states = list(states)
        tiles = [ubuf[s, pl.ds(pl.multiple_of(8 * g, 8), 8), :] for s in range(samples)]
        for i in range(8):
            for s in range(samples):
                states[s] = decay * states[s] + tiles[s][i : i + 1, :]
        return tuple(states)

    zero = jnp.zeros((modes, width), F32)
    features_of(8, block - 8)
    ends = lax.fori_loop(1, block // 8, gather_state, (zero,) * samples)
    rim.wait_recv()
    for s in range(samples):
        ext[s, :8, :] = jnp.where(me == 0, 0.0, ext[s, :8, :])
    features_of(0, 8)
    heads = gather_state(0, (zero,) * samples)
    late = jnp.exp(-rates * float(block - 8))
    for s in range(samples):
        st0[core, s] = late * heads[s] + ends[s]
    pair = remote(st0.at[core], st0.at[core], st0_send, st0_recv, sibling)
    pair.start()

    def fill_table(m, carry):
        rate = rates_ref[pl.ds(m, 1), :]
        steps = lax.broadcasted_iota(jnp.int32, (block, 1), 0).astype(F32) + 1.0
        table[m] = res_ref[pl.ds(m, 1), :] * jnp.sqrt(2.0 * rate / modes) * jnp.exp(-rate * steps)
        return carry

    def convolve(s):
        def body(g, state):
            span = pl.ds(pl.multiple_of(8 * g, 8), 8)
            tile = ubuf[s, span, :]
            lines = []
            for i in range(8):
                state = decay * state + tile[i : i + 1, :]
                lines.append(jnp.sum(coef * state, axis=0, keepdims=True))
            cbuf[s, span, :] = jnp.concatenate(lines, axis=0)
            return state

        lax.fori_loop(0, block // 8, body, zero)

    def sent(s, carry):
        for r, way in lanes:
            for c in range(CHUNKS):
                ag_sent(r, way, s, c)
        return carry

    x_before, x_total = powers(x, 2)
    lax.fori_loop(0, modes, fill_table, 0)
    pair_in = remote(st0.at[1 - core], st0.at[1 - core], st0_send, st0_recv, sibling)
    pair_in.wait_recv()
    for s in range(samples):
        st1[x, s] = whole * st0[0, s] + st0[1, s]
    for j in range(1, side):
        remote(st1.at[x], st1.at[x], st1_send.at[j], st1_recv.at[j], at(y, rem(x + j, side))).start()
    y_before, _ = powers(y, 2 * side)
    x_power = jnp.exp(-rates * (x.astype(F32) * float(2 * block)))
    convolve(0)
    lax.fori_loop(1, half // 2, sent, 0)
    for j in range(1, side):
        slot = st1.at[rem(x + side - j, side)]
        remote(slot, slot, st1_send.at[j], st1_recv.at[j], sibling).wait_recv()
    for s in range(samples):
        st2[y, s] = sum(x_total[i] * st1[i, s] for i in range(side))
    for j in range(1, side):
        remote(st2.at[y], st2.at[y], st2_send.at[j], st2_recv.at[j], at(rem(y + j, side), x)).start()
    convolve(1)
    lax.fori_loop(half // 2, half, sent, 0)
    for r, way in lanes:
        for c in range(CHUNKS):
            if goes_far(way, c):
                ag_sent(r, way, half, c)
    for j in range(1, side):
        slot = st2.at[rem(y + side - j, side)]
        remote(slot, slot, st2_send.at[j], st2_recv.at[j], sibling).wait_recv()
    for s in range(samples):
        row = sum(y_before[i] * st2[i, s] for i in range(side))
        at_chip = x_power * row + sum(x_before[i] * st1[i, s] for i in range(side))
        st_in[s] = jnp.where(core == 0, at_chip, whole * at_chip + st0[0, s])

    tall = 32

    def carry_in(g, carry):
        span = pl.ds(pl.multiple_of(tall * g, tall), tall)
        totals = [cbuf[s, span, :] + skip_ref[...] * ubuf[s, span, :] for s in range(samples)]
        for m in range(modes):
            weight = table[m, span, :]
            for s in range(samples):
                totals[s] = totals[s] + weight * st_in[s, m : m + 1, :]
        for s in range(samples):
            target = pl.ds(pl.multiple_of(block * s + tall * g, tall), tall)
            gated[target, :] = (qbuf[s, span, :] * totals[s]).astype(BF16)
        return carry

    lax.fori_loop(0, block // tall, carry_in, 0)

    def share(d):
        first, second = pbuf[2 * d, :, 3 * width :], pbuf[2 * d + 1, :, 3 * width :]
        right = jnp.concatenate([
            jnp.concatenate([first[:, :rows], second[:, :rows]], axis=1),
            jnp.concatenate([first[:, rows:], second[:, rows:]], axis=1),
        ], axis=0)
        return jnp.dot(gated[...], right, preferred_element_type=F32)

    def rs_copy(way, s, c):
        return remote(
            rs_out.at[way, s - 1, c], rs_in.at[way, s - 1, c],
            rs_send.at[way, s - 1, c], rs_recv.at[way, s - 1, c], rings[0][3][way],
        )

    def prepare(s):
        ahead = half + 1 - s
        parts[RIGHT] = share(rem(z + ahead, n))
        parts[LEFT] = share(rem(z + n - ahead, n))

    def rs_step(s, way, c, first):
        part = parts[way, piece * c : piece * (c + 1), :]
        if not first:
            rs_copy(way, s - 1, c).wait_recv()
            part = part + rs_in[way, s - 2, c].astype(F32)
        rs_out[way, s - 1, c] = part.astype(BF16)
        rs_copy(way, s, c).start()

    order = [(way, c) for far in (False, True) for c in range(CHUNKS) for way in (RIGHT, LEFT) if goes_far(way, c) == far]
    farthest = share(rem(z + half, n))
    for c in range(CHUNKS):
        way = RIGHT if goes_far(RIGHT, c) else LEFT
        rs_out[way, 0, c] = farthest[piece * c : piece * (c + 1), :].astype(BF16)
        rs_copy(way, 1, c).start()
    prepare(2)
    own[...] = share(z) + hraw[z].astype(F32)
    for way, c in order:
        rs_step(2, way, c, not goes_far(way, c))

    for c in range(CHUNKS):
        rs_copy(RIGHT if goes_far(RIGHT, c) else LEFT, 1, c).wait_send()

    def rs_sent(s):
        for way in (RIGHT, LEFT):
            for c in range(CHUNKS):
                rs_copy(way, s, c).wait_send()

    def reduce_step(s, carry):
        prepare(s)
        rs_sent(s - 1)
        for way, c in order:
            rs_step(s, way, c, False)
        return carry

    lax.fori_loop(3, half + 1, reduce_step, 0)
    for c in range(CHUNKS):
        span = slice(piece * c, piece * (c + 1))
        part = own[span, :]
        for way in (RIGHT, LEFT):
            rs_copy(way, half, c).wait_recv()
            part = part + rs_in[way, half - 1, c].astype(F32)
        out_ref[span, :] = part.astype(BF16)

    rim.wait_send()
    pair.wait_send()
    for j in range(1, side):
        remote(st1.at[x], st1.at[x], st1_send.at[j], st1_recv.at[j], sibling).wait_send()
        remote(st2.at[y], st2.at[y], st2_send.at[j], st2_recv.at[j], sibling).wait_send()
    rs_sent(half)


def on_device(hidden, norm_gain, in_weight, short_weight, residues, rates, skip_gain, out_weight, lengths):
    samples, block, width = hidden.shape
    rows = in_weight.shape[0]
    n = lax.axis_size("tp")
    side = int(round(n ** 0.5))
    half = n // 2
    modes = rates.shape[0]
    dma = pltpu.SemaphoreType.DMA
    hbm = pl.BlockSpec(memory_space=pltpu.HBM)
    vmem = pl.BlockSpec(memory_space=pltpu.VMEM)
    state = (samples, modes, width)
    return pl.pallas_call(
        functools.partial(kernel, side),
        out_shape=jax.ShapeDtypeStruct((samples * block, width), BF16),
        in_specs=[hbm] * 8 + [pl.BlockSpec(memory_space=pltpu.SMEM)],
        out_specs=vmem,
        scratch_shapes=[
            pltpu.VMEM((1, n * width), F32),
            pltpu.VMEM(short_weight.shape, F32),
            pltpu.VMEM(rates.shape, F32),
            pltpu.VMEM(rates.shape, F32),
            pltpu.VMEM((1, width), F32),
            pltpu.VMEM((n, samples * block, width), BF16),
            pltpu.VMEM((samples * block, n * width), BF16),
            pltpu.VMEM((2 * n, rows, 3 * width + 2 * rows), BF16),
            pltpu.VMEM((samples * block, width // 2), F32),
            pltpu.VMEM((samples * block, 3 * width), F32),
            pltpu.VMEM((samples, block + 8, 3 * width), F32),
            pltpu.VMEM((samples, block, width), F32),
            pltpu.VMEM((samples, block, width), F32),
            pltpu.VMEM((samples, block, width), F32),
            pltpu.VMEM((samples * block, width), BF16),
            pltpu.VMEM((modes, block, width), F32),
            pltpu.VMEM(state, F32),
            pltpu.VMEM((2,) + state, F32),
            pltpu.VMEM((side,) + state, F32),
            pltpu.VMEM((side,) + state, F32),
            pltpu.VMEM((2, samples * block, width), F32),
            pltpu.VMEM((samples * block, width), F32),
            pltpu.VMEM((2, half, CHUNKS, samples * block // CHUNKS, width), BF16),
            pltpu.VMEM((2, half, CHUNKS, samples * block // CHUNKS, width), BF16),
            dma((11,)),
            dma((3, 2, half, CHUNKS)),
            dma((3, 2, half, CHUNKS)),
            dma((2, 2, half + 1)),
            dma((2, 2, half + 1)),
            dma,
            dma,
            dma,
            dma,
            dma((side,)),
            dma((side,)),
            dma((side,)),
            dma((side,)),
            dma((2, half, CHUNKS)),
            dma((2, half, CHUNKS)),
        ],
        compiler_params=pltpu.CompilerParams(
            collective_id=0, has_side_effects=True, vmem_limit_bytes=60 * 2**20
        ),
    )(
        hidden.reshape(samples * block, width),
        jnp.transpose(in_weight, (1, 0, 2)),
        out_weight,
        norm_gain.reshape(1, n * width),
        short_weight,
        residues,
        rates,
        skip_gain.reshape(1, width),
        lengths,
    ).reshape(hidden.shape)


def solution(mesh):
    placed = (
        P(None, "ctx", "tp"),
        P(),
        P("ctx", None, "tp"),
        P(None, None, "tp"),
        P(None, "tp"),
        P(None, "tp"),
        P("tp"),
        P("tp", "ctx"),
        P(),
    )
    return jax.shard_map(
        on_device, mesh=mesh, in_specs=placed, out_specs=P(None, "ctx", "tp"), check_vma=False
    )
```

```python
import functools

import jax
import jax.numpy as jnp
from jax import lax
from jax.experimental import pallas as pl
from jax.experimental.pallas import tpu as pltpu
from jax.sharding import PartitionSpec as P

MESH = pl.DeviceIdType.MESH
F32, BF16 = jnp.float32, jnp.bfloat16
RIGHT, LEFT = 0, 1
CHUNKS = 4


def rem(a, b):
    return lax.rem(a, jnp.int32(b))


def div(a, b):
    return lax.div(a, jnp.int32(b))


def remote(src, dst, send_sem, recv_sem, device):
    return pltpu.make_async_remote_copy(
        src_ref=src, dst_ref=dst, send_sem=send_sem, recv_sem=recv_sem,
        device_id=device, device_id_type=MESH,
    )


def kernel(
    side, hid_hbm, w_hbm, ow_hbm, gain_hbm, taps_hbm, res_hbm, rates_hbm, skip_hbm, len_ref, out_ref,
    gain_ref, taps_ref, res_ref, rates_ref, skip_ref,
    hraw, hs, pbuf, ssq, acc, ext, qbuf, ubuf, cbuf, gated, table, st_in, st0, st1, st2, parts, rs_out, rs_in,
    load_sem, ag_send, ag_recv, sib_send, sib_recv, rim_send, rim_recv,
    st0_send, st0_recv, st1_send, st1_recv, st2_send, st2_recv, rs_send, rs_recv,
):
    n = side * side
    half = n // 2
    samples, block, width = ubuf.shape
    rows = pbuf.shape[1]
    piece = samples * block // CHUNKS
    modes = rates_ref.shape[0]
    features = n * width
    me = lax.axis_index("ctx")
    z = lax.axis_index("tp")
    core = rem(me, 2)
    chip = div(me, 2)
    y, x = div(chip, side), rem(chip, side)
    turn = rem(x + y, side)
    sibling = {"ctx": me + 1 - 2 * core}

    def at(yy, xx):
        return {"ctx": 2 * (side * yy + xx) + core}

    def chip_first(q):
        a = div(q, side)
        return side * a + rem(q - side * a + side - a, side)

    def chip_second(q):
        a = div(q, side)
        return side * rem(q - side * a + side - a, side) + a

    def from_last(steps):
        return rem(me + 2 * n - steps, 2 * n)

    quarter = rows // CHUNKS
    columns = (pl.ds(0, 3 * width), pl.ds(3 * width, 2 * rows))

    first_place, second_place = side * y + turn, side * x + turn

    def ring(place, slot, device, chunk):
        return place, slot, chunk, (device(rem(place + 1, n)), device(rem(place + n - 1, n)))

    def first_slot(q):
        return 2 * chip_first(q) + core

    def second_slot(q):
        return 2 * chip_second(q) + core

    rings = [
        ring(z, lambda q: q, lambda q: {"tp": q}, lambda at_slot, c: hraw.at[at_slot, pl.ds(piece * c, piece)]),
        ring(
            first_place, first_slot, lambda q: {"ctx": first_slot(q)},
            lambda at_slot, c: pbuf.at[at_slot, pl.ds(quarter * (c % 2), quarter), columns[c // 2]],
        ),
        ring(
            second_place, second_slot, lambda q: {"ctx": second_slot(q)},
            lambda at_slot, c: pbuf.at[at_slot, pl.ds(rows // 2 + quarter * (c % 2), quarter), columns[c // 2]],
        ),
    ]

    def slot_of(r, way, s):
        place, slot = rings[r][:2]
        return slot(rem(place + n - s, n) if way == RIGHT else rem(place + s, n))

    def ag_copy(r, way, s, c, at_slot):
        part = rings[r][2](at_slot, c)
        return remote(part, part, ag_send.at[r, way, s - 1, c], ag_recv.at[r, way, s - 1, c], rings[r][3][way])

    def ag_start(r, way, s, c, at_slot):
        ag_copy(r, way, s, c, at_slot).start()

    def ag_arrived(r, way, s, c):
        ag_copy(r, way, s, c, 0).wait_recv()

    def ag_sent(r, way, s, c):
        ag_copy(r, way, s, c, 0).wait_send()

    def sib_copy(phase, r, way, s, at_slot):
        part = pbuf.at[at_slot, pl.ds(rows // 2 * (r - 1), rows // 2), columns[phase]]
        return remote(part, part, sib_send.at[phase, r - 1, way, s], sib_recv.at[phase, r - 1, way, s], sibling)

    def sib_wait(phase, r, way, s):
        copy = sib_copy(phase, r, way, s, 0)
        copy.wait_send()
        copy.wait_recv()

    loads = [pltpu.make_async_copy(hid_hbm, hraw.at[z], load_sem.at[0])]
    for j in range(3):
        loads.append(pltpu.make_async_copy(
            w_hbm.at[j], pbuf.at[me, :, pl.ds(width * j, width)], load_sem.at[1 + j]))
    for j in range(2):
        loads.append(pltpu.make_async_copy(
            ow_hbm.at[pl.ds(rows * j, rows)], pbuf.at[me, :, pl.ds(3 * width + rows * j, rows)], load_sem.at[4 + j]))
    small = [(gain_hbm, gain_ref), (taps_hbm, taps_ref), (res_hbm, res_ref), (rates_hbm, rates_ref), (skip_hbm, skip_ref)]
    for j, (source, target) in enumerate(small):
        loads.append(pltpu.make_async_copy(source, target, load_sem.at[6 + j]))
    for copy in loads:
        copy.start()
    partners = [{"tp": rem(z + 1, n)}, {"tp": rem(z + n - 1, n)}, sibling, {"ctx": from_last(1)}]
    for j in range(1, side):
        partners.append(at(y, rem(x + j, side)))
        partners.append(at(rem(y + j, side), x))
    barrier = pltpu.get_barrier_semaphore()
    for partner in partners:
        pl.semaphore_signal(barrier, inc=1, device_id=partner, device_id_type=MESH)
    for copy in loads:
        copy.wait()
    pl.semaphore_wait(barrier, len(partners))

    def take(q, s):
        gain = gain_ref[:, pl.ds(pl.multiple_of(q * width, width), width)]
        span = pl.ds(s * block, block)
        value = hraw[q, span, :].astype(F32)
        square = value * value
        ssq[span, :] = ssq[span, :] + square[:, : width // 2] + square[:, width // 2 :]
        hs[span, pl.ds(pl.multiple_of(q * width, width), width)] = (value * gain).astype(BF16)

    def goes_far(way, c):
        return (c % 2 == 0) == (way == RIGHT)

    lanes = [(r, way) for r in range(3) for way in (RIGHT, LEFT)]
    mine = [z, me, me]

    def ag_begin(phase):
        for c in (2 * phase, 2 * phase + 1):
            for r, way in lanes:
                ag_start(r, way, 1, c, mine[r])

    def ag_step(phase, s, last):
        slots = {(r, way): slot_of(r, way, s) for r, way in lanes}
        for c in (2 * phase, 2 * phase + 1):
            for r, way in lanes:
                ag_arrived(r, way, s, c)
                if not last or goes_far(way, c):
                    ag_start(r, way, s + 1, c, slots[r, way])
        for r, way in lanes[2:]:
            sib_copy(phase, r, way, s, slots[r, way]).start()
        take(slots[0, RIGHT], phase)
        take(slots[0, LEFT], phase)

    def ag_end(phase):
        for r in (1, 2, 0):
            for c in (2 * phase, 2 * phase + 1):
                ag_arrived(r, RIGHT if goes_far(RIGHT, c) else LEFT, half, c)
            if r:
                sib_copy(phase, r, RIGHT, half, slot_of(r, RIGHT, half)).start()
        take(slot_of(0, RIGHT, half), phase)

    def sib_end(phase):
        def step(s, carry):
            for r in (1, 2):
                for way in (RIGHT, LEFT):
                    sib_wait(phase, r, way, s)
            return carry

        lax.fori_loop(1, half, step, 0)
        for r in (1, 2):
            sib_wait(phase, r, RIGHT, 0)
            sib_wait(phase, r, RIGHT, half)

    ag_begin(0)
    for phase in range(2):
        for r in (1, 2):
            sib_copy(phase, r, RIGHT, 0, me).start()
    ssq[...] = jnp.zeros_like(ssq)
    take(z, 0)
    take(z, 1)

    def first_phase(s, carry):
        ag_step(0, s, False)
        return carry

    lax.fori_loop(1, half - 1, first_phase, 0)
    ag_step(0, half - 1, True)
    ag_begin(1)
    ag_end(0)
    sib_end(0)

    deep = 4 if n % 4 == 0 else 1
    span_k = deep * width

    def project(s, i):
        span = pl.ds(s * block, block)
        per = span_k // rows
        left = hs[span, i * span_k : (i + 1) * span_k]
        right = pbuf[i * per : (i + 1) * per, :, : 3 * width].reshape(span_k, 3 * width)
        product = jnp.dot(left, right, preferred_element_type=F32)
        acc[span, :] = product if i == 0 else acc[span, :] + product

    def rim_copy(s):
        return remote(
            ext.at[s, pl.ds(block, 8)], ext.at[s, pl.ds(0, 8)], rim_send.at[s], rim_recv.at[s],
            {"ctx": rem(me + 1, 2 * n)},
        )

    def normalize(s):
        span = pl.ds(s * block, block)
        mean = jnp.sum(ssq[span, :], axis=1, keepdims=True) * (1.0 / features)
        ext[s, 8:, :] = acc[span, :] * lax.rsqrt(mean + 1e-6)
        rim_copy(s).start()

    rates = rates_ref[...]
    decay = jnp.exp(-rates)
    whole = jnp.exp(-rates * float(block))
    coef = res_ref[...] * jnp.sqrt(2.0 * rates / modes)

    def powers(place, blocks):
        before, total = [], []
        for i in range(side):
            gap = jnp.maximum(place - 1 - i, 0).astype(F32)
            factor = jnp.exp(-rates * (gap * float(blocks * block)))
            before.append(jnp.where(i < place, factor, 0.0))
            total.append(jnp.exp(-rates * float(blocks * block * (side - 1 - i))))
        return before, total

    def filtered(s, j, first, count):
        total = None
        for i in range(3):
            term = taps_ref[i, j : j + 1, :] * ext[s, 8 + first - i : 8 + first - i + count, j * width : (j + 1) * width]
            total = term if total is None else total + term
        return total

    def features_of(s, first, count):
        place = lax.broadcasted_iota(jnp.int32, (count, 1), 0) + (me * block + first)
        valid = jnp.where(place < len_ref[s], 1.0, 0.0)
        span = slice(first, first + count)
        pushed = filtered(s, 1, first, count) * filtered(s, 2, first, count) * valid
        ubuf[s, span, :] = pushed.astype(BF16).astype(F32)
        qbuf[s, span, :] = filtered(s, 0, first, count) * valid

    zero = jnp.zeros((modes, width), F32)

    def add_states(s, first, last):
        def body(g, state):
            tile = ubuf[s, pl.ds(pl.multiple_of(8 * g, 8), 8), :]
            for i in range(8):
                state = decay * state + tile[i : i + 1, :]
            return state

        return lax.fori_loop(first, last, body, zero)

    def pair_copy(s, which):
        return remote(st0.at[which, s], st0.at[which, s], st0_send.at[s], st0_recv.at[s], sibling)

    def x_copy(s, j, slot, to):
        return remote(st1.at[slot, s], st1.at[slot, s], st1_send.at[s, j], st1_recv.at[s, j], to)

    def y_copy(s, j, slot, to):
        return remote(st2.at[slot, s], st2.at[slot, s], st2_send.at[s, j], st2_recv.at[s, j], to)

    def tail_state(s):
        features_of(s, 8, block - 8)
        st_in[s] = add_states(s, 1, block // 8)

    def end_state(s):
        rim_copy(s).wait_recv()
        ext[s, :8, :] = jnp.where(me == 0, 0.0, ext[s, :8, :])
        features_of(s, 0, 8)
        st0[core, s] = jnp.exp(-rates * float(block - 8)) * add_states(s, 0, 1) + st_in[s]
        pair_copy(s, core).start()

    def fill_table():
        def body(m, carry):
            rate = rates_ref[pl.ds(m, 1), :]
            steps = lax.broadcasted_iota(jnp.int32, (block, 1), 0).astype(F32) + 1.0
            table[m] = res_ref[pl.ds(m, 1), :] * jnp.sqrt(2.0 * rate / modes) * jnp.exp(-rate * steps)
            return carry

        lax.fori_loop(0, modes, body, 0)

    def convolve(s):
        def body(g, state):
            span = pl.ds(pl.multiple_of(8 * g, 8), 8)
            tile = ubuf[s, span, :]
            lines = []
            for i in range(8):
                state = decay * state + tile[i : i + 1, :]
                lines.append(jnp.sum(coef * state, axis=0, keepdims=True))
            cbuf[s, span, :] = jnp.concatenate(lines, axis=0)
            return state

        lax.fori_loop(0, block // 8, body, zero)

    def to_row(s):
        pair_copy(s, 1 - core).wait_recv()
        st1[x, s] = whole * st0[0, s] + st0[1, s]
        for j in range(1, side):
            x_copy(s, j, x, at(y, rem(x + j, side))).start()

    def to_column(s):
        for j in range(1, side):
            x_copy(s, j, rem(x + side - j, side), sibling).wait_recv()
        _, x_total = powers(x, 2)
        st2[y, s] = sum(x_total[i] * st1[i, s] for i in range(side))
        for j in range(1, side):
            y_copy(s, j, y, at(rem(y + j, side), x)).start()

    tall = 32

    def gate(s):
        x_before, _ = powers(x, 2)
        y_before, _ = powers(y, 2 * side)
        x_power = jnp.exp(-rates * (x.astype(F32) * float(2 * block)))
        for j in range(1, side):
            y_copy(s, j, rem(y + side - j, side), sibling).wait_recv()
        row = sum(y_before[i] * st2[i, s] for i in range(side))
        at_chip = x_power * row + sum(x_before[i] * st1[i, s] for i in range(side))
        st_in[s] = jnp.where(core == 0, at_chip, whole * at_chip + st0[0, s])

        def body(g, carry):
            span = pl.ds(pl.multiple_of(tall * g, tall), tall)
            total = cbuf[s, span, :] + skip_ref[...] * ubuf[s, span, :]
            for m in range(modes):
                total = total + table[m, span, :] * st_in[s, m : m + 1, :]
            target = pl.ds(pl.multiple_of(block * s + tall * g, tall), tall)
            gated[target, :] = (qbuf[s, span, :] * total).astype(BF16)
            return carry

        lax.fori_loop(0, block // tall, body, 0)

    def share(d, s):
        first, second = pbuf[2 * d, :, 3 * width :], pbuf[2 * d + 1, :, 3 * width :]
        right = jnp.concatenate([
            jnp.concatenate([first[:, :rows], second[:, :rows]], axis=1),
            jnp.concatenate([first[:, rows:], second[:, rows:]], axis=1),
        ], axis=0)
        return jnp.dot(gated[block * s : block * (s + 1), :], right, preferred_element_type=F32)

    def rs_copy(way, s, c):
        return remote(
            rs_out.at[way, s - 1, c], rs_in.at[way, s - 1, c],
            rs_send.at[way, s - 1, c], rs_recv.at[way, s - 1, c], rings[0][3][way],
        )

    def prepare(sample, s):
        ahead = half + 1 - s
        span = slice(block * sample, block * (sample + 1))
        parts[RIGHT, span, :] = share(rem(z + ahead, n), sample)
        parts[LEFT, span, :] = share(rem(z + n - ahead, n), sample)

    def rs_send_on(s, way, c, first):
        part = parts[way, piece * c : piece * (c + 1), :]
        if not first:
            rs_copy(way, s - 1, c).wait_recv()
            part = part + rs_in[way, s - 2, c].astype(F32)
        rs_out[way, s - 1, c] = part.astype(BF16)
        rs_copy(way, s, c).start()

    def order(sample):
        return [(RIGHT, 2 * sample + 1), (LEFT, 2 * sample), (RIGHT, 2 * sample), (LEFT, 2 * sample + 1)]

    def rs_begin(sample):
        farthest = share(rem(z + half, n), sample)
        for i, way in enumerate((RIGHT, LEFT)):
            c = 2 * sample + i
            rs_out[way, 0, c] = farthest[piece * i : piece * (i + 1), :].astype(BF16)
            rs_copy(way, 1, c).start()
        prepare(sample, 2)
        for way, c in order(sample):
            rs_send_on(2, way, c, not goes_far(way, c))

    def rs_step(sample, s):
        prepare(sample, s)
        for way, c in order(sample):
            rs_send_on(s, way, c, False)

    def rs_end(sample):
        own = share(z, sample)
        for i in range(2):
            c = 2 * sample + i
            span = slice(piece * c, piece * (c + 1))
            part = own[piece * i : piece * (i + 1), :] + hraw[z, span, :].astype(F32)
            for way in (RIGHT, LEFT):
                rs_copy(way, half, c).wait_recv()
                part = part + rs_in[way, half - 1, c].astype(F32)
            out_ref[span, :] = part.astype(BF16)

    def work(s):
        def run(f, *more):
            return lambda: f(s, *more)

        jobs = [run(project, i) for i in range(n // deep)]
        jobs += [run(normalize), run(tail_state), run(end_state)]
        jobs += [fill_table] if s == 0 else []
        return jobs + [run(to_row), run(convolve), run(to_column), run(gate)]

    def interleave(jobs, steps):
        for i in range(max(len(jobs), len(steps))):
            if i < len(jobs):
                jobs[i]()
            if i < len(steps):
                steps[i]()

    steps = [functools.partial(ag_step, 1, s, s == half - 1) for s in range(1, half)] + [lambda: ag_end(1)]
    interleave(work(0), steps)
    sib_end(1)
    rs_begin(0)
    interleave(work(1), [functools.partial(rs_step, 0, s) for s in range(3, half + 1)])
    rs_begin(1)
    rs_end(0)

    def reduce_step(s, carry):
        rs_step(1, s)
        return carry

    lax.fori_loop(3, half + 1, reduce_step, 0)
    rs_end(1)

    def sent(s, carry):
        for r, way in lanes:
            for c in range(CHUNKS):
                ag_sent(r, way, s, c)
        return carry

    lax.fori_loop(1, half, sent, 0)
    for r, way in lanes:
        for c in range(CHUNKS):
            if goes_far(way, c):
                ag_sent(r, way, half, c)
    for s in range(samples):
        rim_copy(s).wait_send()
        pair_copy(s, core).wait_send()
        for j in range(1, side):
            x_copy(s, j, x, sibling).wait_send()
            y_copy(s, j, y, sibling).wait_send()

    def reduced(s, carry):
        for way in (RIGHT, LEFT):
            for c in range(CHUNKS):
                rs_copy(way, s, c).wait_send()
        return carry

    lax.fori_loop(2, half + 1, reduced, 0)
    for c in range(CHUNKS):
        rs_copy(RIGHT if goes_far(RIGHT, c) else LEFT, 1, c).wait_send()


def on_device(hidden, norm_gain, in_weight, short_weight, residues, rates, skip_gain, out_weight, lengths):
    samples, block, width = hidden.shape
    rows = in_weight.shape[0]
    n = lax.axis_size("tp")
    side = int(round(n ** 0.5))
    half = n // 2
    modes = rates.shape[0]
    dma = pltpu.SemaphoreType.DMA
    hbm = pl.BlockSpec(memory_space=pltpu.HBM)
    vmem = pl.BlockSpec(memory_space=pltpu.VMEM)
    state = (samples, modes, width)
    return pl.pallas_call(
        functools.partial(kernel, side),
        out_shape=jax.ShapeDtypeStruct((samples * block, width), BF16),
        in_specs=[hbm] * 8 + [pl.BlockSpec(memory_space=pltpu.SMEM)],
        out_specs=vmem,
        scratch_shapes=[
            pltpu.VMEM((1, n * width), F32),
            pltpu.VMEM(short_weight.shape, F32),
            pltpu.VMEM(rates.shape, F32),
            pltpu.VMEM(rates.shape, F32),
            pltpu.VMEM((1, width), F32),
            pltpu.VMEM((n, samples * block, width), BF16),
            pltpu.VMEM((samples * block, n * width), BF16),
            pltpu.VMEM((2 * n, rows, 3 * width + 2 * rows), BF16),
            pltpu.VMEM((samples * block, width // 2), F32),
            pltpu.VMEM((samples * block, 3 * width), F32),
            pltpu.VMEM((samples, block + 8, 3 * width), F32),
            pltpu.VMEM((samples, block, width), F32),
            pltpu.VMEM((samples, block, width), F32),
            pltpu.VMEM((samples, block, width), F32),
            pltpu.VMEM((samples * block, width), BF16),
            pltpu.VMEM((modes, block, width), F32),
            pltpu.VMEM(state, F32),
            pltpu.VMEM((2,) + state, F32),
            pltpu.VMEM((side,) + state, F32),
            pltpu.VMEM((side,) + state, F32),
            pltpu.VMEM((2, samples * block, width), F32),
            pltpu.VMEM((2, half, CHUNKS, samples * block // CHUNKS, width), BF16),
            pltpu.VMEM((2, half, CHUNKS, samples * block // CHUNKS, width), BF16),
            dma((11,)),
            dma((3, 2, half, CHUNKS)),
            dma((3, 2, half, CHUNKS)),
            dma((2, 2, 2, half + 1)),
            dma((2, 2, 2, half + 1)),
            dma((samples,)),
            dma((samples,)),
            dma((samples,)),
            dma((samples,)),
            dma((samples, side)),
            dma((samples, side)),
            dma((samples, side)),
            dma((samples, side)),
            dma((2, half, CHUNKS)),
            dma((2, half, CHUNKS)),
        ],
        compiler_params=pltpu.CompilerParams(
            collective_id=0, has_side_effects=True, vmem_limit_bytes=60 * 2**20
        ),
    )(
        hidden.reshape(samples * block, width),
        jnp.transpose(in_weight, (1, 0, 2)),
        out_weight,
        norm_gain.reshape(1, n * width),
        short_weight,
        residues,
        rates,
        skip_gain.reshape(1, width),
        lengths,
    ).reshape(hidden.shape)


def solution(mesh):
    placed = (
        P(None, "ctx", "tp"),
        P(),
        P("ctx", None, "tp"),
        P(None, None, "tp"),
        P(None, "tp"),
        P(None, "tp"),
        P("tp"),
        P("tp", "ctx"),
        P(),
    )
    return jax.shard_map(
        on_device, mesh=mesh, in_specs=placed, out_specs=P(None, "ctx", "tp"), check_vma=False
    )
```

```python
import functools

import jax
import jax.numpy as jnp
from jax import lax
from jax.experimental import pallas as pl
from jax.experimental.pallas import tpu as pltpu
from jax.sharding import PartitionSpec as P

MESH = pl.DeviceIdType.MESH
F32, BF16 = jnp.float32, jnp.bfloat16
RIGHT, LEFT = 0, 1
CHUNKS = 4


def rem(a, b):
    return lax.rem(a, jnp.int32(b))


def div(a, b):
    return lax.div(a, jnp.int32(b))


def remote(src, dst, send_sem, recv_sem, device):
    return pltpu.make_async_remote_copy(
        src_ref=src, dst_ref=dst, send_sem=send_sem, recv_sem=recv_sem,
        device_id=device, device_id_type=MESH,
    )


def kernel(
    side, hid_hbm, w_hbm, ow_hbm, gain_hbm, taps_hbm, res_hbm, rates_hbm, skip_hbm, len_ref, out_ref,
    gain_ref, taps_ref, res_ref, rates_ref, skip_ref,
    hraw, hs, pbuf, ssq, acc, ext, qbuf, ubuf, cbuf, gated, table, st_in, st1, st2, parts, rs_out, rs_in,
    load_sem, ag_send, ag_recv, sib_send, sib_recv, rim_send, rim_recv,
    st1_send, st1_recv, st2_send, st2_recv, rs_send, rs_recv,
):
    n = side * side
    half = n // 2
    samples, block, width = ubuf.shape
    rows = pbuf.shape[1]
    piece = samples * block // CHUNKS
    modes = rates_ref.shape[0]
    features = n * width
    me = lax.axis_index("ctx")
    z = lax.axis_index("tp")
    core = rem(me, 2)
    chip = div(me, 2)
    y, x = div(chip, side), rem(chip, side)
    turn = rem(x + y, side)
    sibling = {"ctx": me + 1 - 2 * core}

    def at(yy, xx):
        return {"ctx": 2 * (side * yy + xx) + core}

    place = rem(me, 2 * side)

    def in_row(steps):
        return {"ctx": me - place + rem(place + steps, 2 * side)}

    def chip_first(q):
        a = div(q, side)
        return side * a + rem(q - side * a + side - a, side)

    def chip_second(q):
        a = div(q, side)
        return side * rem(q - side * a + side - a, side) + a

    def from_last(steps):
        return rem(me + 2 * n - steps, 2 * n)

    quarter = rows // (2 * CHUNKS)
    first_place, second_place = side * y + turn, side * x + turn

    def ring(place, slot, device, chunk):
        return place, slot, chunk, (device(rem(place + 1, n)), device(rem(place + n - 1, n)))

    def first_slot(q):
        return 2 * chip_first(q) + core

    def second_slot(q):
        return 2 * chip_second(q) + core

    rings = [
        ring(z, lambda q: q, lambda q: {"tp": q}, lambda at_slot, c: hraw.at[at_slot, pl.ds(piece * c, piece)]),
        ring(
            first_place, first_slot, lambda q: {"ctx": first_slot(q)},
            lambda at_slot, c: pbuf.at[at_slot, pl.ds(quarter * c, quarter)],
        ),
        ring(
            second_place, second_slot, lambda q: {"ctx": second_slot(q)},
            lambda at_slot, c: pbuf.at[at_slot, pl.ds(rows // 2 + quarter * c, quarter)],
        ),
    ]

    def slot_of(r, way, s):
        spot, slot = rings[r][:2]
        return slot(rem(spot + n - s, n) if way == RIGHT else rem(spot + s, n))

    def ag_copy(r, way, s, c, at_slot):
        part = rings[r][2](at_slot, c)
        return remote(part, part, ag_send.at[r, way, s - 1, c], ag_recv.at[r, way, s - 1, c], rings[r][3][way])

    def ag_start(r, way, s, c, at_slot):
        ag_copy(r, way, s, c, at_slot).start()

    def ag_arrived(r, way, s, c):
        ag_copy(r, way, s, c, 0).wait_recv()

    def ag_sent(r, way, s, c):
        ag_copy(r, way, s, c, 0).wait_send()

    def sib_copy(r, way, s, at_slot):
        part = pbuf.at[at_slot, pl.ds(rows // 2 * (r - 1), rows // 2)]
        return remote(part, part, sib_send.at[r - 1, way, s], sib_recv.at[r - 1, way, s], sibling)

    def sib_wait(r, way, s):
        copy = sib_copy(r, way, s, 0)
        copy.wait_send()
        copy.wait_recv()

    loads = [pltpu.make_async_copy(hid_hbm, hraw.at[z], load_sem.at[0])]
    for j in range(3):
        loads.append(pltpu.make_async_copy(
            w_hbm.at[j], pbuf.at[me, :, pl.ds(width * j, width)], load_sem.at[1 + j]))
    for j in range(2):
        loads.append(pltpu.make_async_copy(
            ow_hbm.at[pl.ds(rows * j, rows)], pbuf.at[me, :, pl.ds(3 * width + rows * j, rows)], load_sem.at[4 + j]))
    small = [(gain_hbm, gain_ref), (taps_hbm, taps_ref), (res_hbm, res_ref), (rates_hbm, rates_ref), (skip_hbm, skip_ref)]
    for j, (source, target) in enumerate(small):
        loads.append(pltpu.make_async_copy(source, target, load_sem.at[6 + j]))
    for copy in loads:
        copy.start()
    partners = [{"tp": rem(z + 1, n)}, {"tp": rem(z + n - 1, n)}, {"ctx": from_last(1)}]
    partners += [in_row(j) for j in range(1, 2 * side)]
    partners += [at(rem(y + j, side), x) for j in range(1, side)]
    barrier = pltpu.get_barrier_semaphore()
    for partner in partners:
        pl.semaphore_signal(barrier, inc=1, device_id=partner, device_id_type=MESH)
    for copy in loads:
        copy.wait()
    pl.semaphore_wait(barrier, len(partners))

    def take(q):
        gain = gain_ref[:, pl.ds(pl.multiple_of(q * width, width), width)]
        for s in range(samples):
            value = hraw[q, s * block : (s + 1) * block, :].astype(F32)
            span = pl.ds(s * block, block)
            square = value * value
            ssq[span, :] = ssq[span, :] + square[:, : width // 2] + square[:, width // 2 :]
            hs[span, pl.ds(pl.multiple_of(q * width, width), width)] = (value * gain).astype(BF16)

    def goes_far(way, c):
        return (c < CHUNKS // 2) == (way == RIGHT)

    lanes = [(r, way) for r in range(3) for way in (RIGHT, LEFT)]
    mine = [z, me, me]
    for c in range(CHUNKS):
        for r, way in lanes:
            ag_start(r, way, 1, c, mine[r])
    for r in (1, 2):
        sib_copy(r, RIGHT, 0, me).start()
    ssq[...] = jnp.zeros_like(ssq)
    take(z)

    def ag_step(s, carry):
        slots = {(r, way): slot_of(r, way, s) for r, way in lanes}
        for c in range(CHUNKS):
            for r, way in lanes:
                ag_arrived(r, way, s, c)
                ag_start(r, way, s + 1, c, slots[r, way])
        for r, way in lanes[2:]:
            sib_copy(r, way, s, slots[r, way]).start()
        take(slots[0, RIGHT])
        take(slots[0, LEFT])
        return carry

    lax.fori_loop(1, half - 1, ag_step, 0)
    slots = {(r, way): slot_of(r, way, half - 1) for r, way in lanes}
    for c in range(CHUNKS):
        for r, way in lanes:
            ag_arrived(r, way, half - 1, c)
            if goes_far(way, c):
                ag_start(r, way, half, c, slots[r, way])
    for r, way in lanes[2:]:
        sib_copy(r, way, half - 1, slots[r, way]).start()
    take(slots[0, RIGHT])
    take(slots[0, LEFT])
    for r in (1, 2, 0):
        for c in range(CHUNKS):
            ag_arrived(r, RIGHT if goes_far(RIGHT, c) else LEFT, half, c)
        if r:
            sib_copy(r, RIGHT, half, slot_of(r, RIGHT, half)).start()
    take(slot_of(0, RIGHT, half))
    for r in (1, 2):
        sib_wait(r, RIGHT, 0)

    def sib_step(s, carry):
        for r in (1, 2):
            for way in (RIGHT, LEFT):
                sib_wait(r, way, s)
        return carry

    lax.fori_loop(1, half, sib_step, 0)

    span_k = side * width
    per = span_k // rows

    def product(steps):
        i = rem(y + steps, side)
        left = hs[:, pl.ds(pl.multiple_of(i * span_k, span_k), span_k)]
        right = pbuf[pl.ds(i * per, per), :, : 3 * width].reshape(span_k, 3 * width)
        return jnp.dot(left, right, preferred_element_type=F32)

    acc[...] = product(0)
    for steps in range(1, side):
        if steps != side // 2:
            acc[...] = acc[...] + product(steps)
    for r in (1, 2):
        sib_wait(r, RIGHT, half)
    acc[...] = acc[...] + product(side // 2)
    mean = jnp.sum(ssq[...], axis=1, keepdims=True) * (1.0 / features)
    scale = lax.rsqrt(mean + 1e-6)
    for s in range(samples):
        ext[s, 8:, :] = acc[s * block : (s + 1) * block, :] * scale[s * block : (s + 1) * block, :]
    rim = remote(ext.at[:, pl.ds(block, 8)], ext.at[:, pl.ds(0, 8)], rim_send, rim_recv, {"ctx": rem(me + 1, 2 * n)})
    rim.start()

    rates = rates_ref[...]
    decay = jnp.exp(-rates)
    coef = res_ref[...] * jnp.sqrt(2.0 * rates / modes)

    def powers(spot, blocks, count):
        before, total = [], []
        for i in range(count):
            gap = jnp.maximum(spot - 1 - i, 0).astype(F32)
            factor = jnp.exp(-rates * (gap * float(blocks * block)))
            before.append(jnp.where(i < spot, factor, 0.0))
            total.append(jnp.exp(-rates * float(blocks * block * (count - 1 - i))))
        return before, total

    def filtered(s, j, first, count):
        total = None
        for i in range(3):
            term = taps_ref[i, j : j + 1, :] * ext[s, 8 + first - i : 8 + first - i + count, j * width : (j + 1) * width]
            total = term if total is None else total + term
        return total

    def features_of(first, count):
        for s in range(samples):
            position = lax.broadcasted_iota(jnp.int32, (count, 1), 0) + (me * block + first)
            valid = jnp.where(position < len_ref[s], 1.0, 0.0)
            span = slice(first, first + count)
            pushed = filtered(s, 1, first, count) * filtered(s, 2, first, count) * valid
            ubuf[s, span, :] = pushed.astype(BF16).astype(F32)
            qbuf[s, span, :] = filtered(s, 0, first, count) * valid

    def gather_state(g, states):
        states = list(states)
        tiles = [ubuf[s, pl.ds(pl.multiple_of(8 * g, 8), 8), :] for s in range(samples)]
        for i in range(8):
            for s in range(samples):
                states[s] = decay * states[s] + tiles[s][i : i + 1, :]
        return tuple(states)

    zero = jnp.zeros((modes, width), F32)
    features_of(8, block - 8)
    ends = lax.fori_loop(1, block // 8, gather_state, (zero,) * samples)
    rim.wait_recv()
    for s in range(samples):
        ext[s, :8, :] = jnp.where(me == 0, 0.0, ext[s, :8, :])
    features_of(0, 8)
    heads = gather_state(0, (zero,) * samples)
    late = jnp.exp(-rates * float(block - 8))
    for s in range(samples):
        st1[place, s] = late * heads[s] + ends[s]
    for j in range(1, 2 * side):
        remote(st1.at[place], st1.at[place], st1_send.at[j], st1_recv.at[j], in_row(j)).start()

    def fill_table(m, carry):
        rate = rates_ref[pl.ds(m, 1), :]
        steps = lax.broadcasted_iota(jnp.int32, (block, 1), 0).astype(F32) + 1.0
        table[m] = res_ref[pl.ds(m, 1), :] * jnp.sqrt(2.0 * rate / modes) * jnp.exp(-rate * steps)
        return carry

    def convolve(s):
        def body(g, state):
            span = pl.ds(pl.multiple_of(8 * g, 8), 8)
            tile = ubuf[s, span, :]
            lines = []
            for i in range(8):
                state = decay * state + tile[i : i + 1, :]
                lines.append(jnp.sum(coef * state, axis=0, keepdims=True))
            cbuf[s, span, :] = jnp.concatenate(lines, axis=0)
            return state

        lax.fori_loop(0, block // 8, body, zero)

    x_before, x_total = powers(place, 1, 2 * side)
    lax.fori_loop(0, modes, fill_table, 0)
    convolve(0)
    for j in range(1, 2 * side):
        slot = st1.at[rem(place + 2 * side - j, 2 * side)]
        remote(slot, slot, st1_send.at[j], st1_recv.at[j], sibling).wait_recv()
    for s in range(samples):
        st2[y, s] = sum(x_total[i] * st1[i, s] for i in range(2 * side))
    for j in range(1, side):
        remote(st2.at[y], st2.at[y], st2_send.at[j], st2_recv.at[j], at(rem(y + j, side), x)).start()
    y_before, _ = powers(y, 2 * side, side)
    x_power = jnp.exp(-rates * (place.astype(F32) * float(block)))
    convolve(1)
    for j in range(1, side):
        slot = st2.at[rem(y + side - j, side)]
        remote(slot, slot, st2_send.at[j], st2_recv.at[j], sibling).wait_recv()
    for s in range(samples):
        row = sum(y_before[i] * st2[i, s] for i in range(side))
        st_in[s] = x_power * row + sum(x_before[i] * st1[i, s] for i in range(2 * side))

    tall = 32

    def carry_in(g, carry):
        span = pl.ds(pl.multiple_of(tall * g, tall), tall)
        totals = [cbuf[s, span, :] + skip_ref[...] * ubuf[s, span, :] for s in range(samples)]
        for m in range(modes):
            weight = table[m, span, :]
            for s in range(samples):
                totals[s] = totals[s] + weight * st_in[s, m : m + 1, :]
        for s in range(samples):
            target = pl.ds(pl.multiple_of(block * s + tall * g, tall), tall)
            gated[target, :] = (qbuf[s, span, :] * totals[s]).astype(BF16)
        return carry

    lax.fori_loop(0, block // tall, carry_in, 0)

    def share(d):
        first, second = pbuf[2 * d, :, 3 * width :], pbuf[2 * d + 1, :, 3 * width :]
        right = jnp.concatenate([
            jnp.concatenate([first[:, :rows], second[:, :rows]], axis=1),
            jnp.concatenate([first[:, rows:], second[:, rows:]], axis=1),
        ], axis=0)
        return jnp.dot(gated[...], right, preferred_element_type=F32)

    def rs_copy(way, s, c):
        return remote(
            rs_out.at[way, s - 1, c], rs_in.at[way, s - 1, c],
            rs_send.at[way, s - 1, c], rs_recv.at[way, s - 1, c], rings[0][3][way],
        )

    def prepare(s):
        ahead = half + 1 - s
        parts[RIGHT] = share(rem(z + ahead, n))
        parts[LEFT] = share(rem(z + n - ahead, n))

    def rs_step(s, way, c, first):
        part = parts[way, piece * c : piece * (c + 1), :]
        if not first:
            rs_copy(way, s - 1, c).wait_recv()
            part = part + rs_in[way, s - 2, c].astype(F32)
        rs_out[way, s - 1, c] = part.astype(BF16)
        rs_copy(way, s, c).start()

    order = [(way, c) for far in (False, True) for c in range(CHUNKS) for way in (RIGHT, LEFT) if goes_far(way, c) == far]
    farthest = share(rem(z + half, n))
    for c in range(CHUNKS):
        way = RIGHT if goes_far(RIGHT, c) else LEFT
        rs_out[way, 0, c] = farthest[piece * c : piece * (c + 1), :].astype(BF16)
        rs_copy(way, 1, c).start()
    prepare(2)
    for way, c in order:
        rs_step(2, way, c, not goes_far(way, c))

    def reduce_step(s, carry):
        prepare(s)
        for way, c in order:
            rs_step(s, way, c, False)
        return carry

    lax.fori_loop(3, half + 1, reduce_step, 0)
    own = share(z)
    for c in range(CHUNKS):
        span = slice(piece * c, piece * (c + 1))
        part = own[span, :] + hraw[z, span, :].astype(F32)
        for way in (RIGHT, LEFT):
            rs_copy(way, half, c).wait_recv()
            part = part + rs_in[way, half - 1, c].astype(F32)
        out_ref[span, :] = part.astype(BF16)

    def sent(s, carry):
        for r, way in lanes:
            for c in range(CHUNKS):
                ag_sent(r, way, s, c)
        return carry

    lax.fori_loop(1, half, sent, 0)
    for r, way in lanes:
        for c in range(CHUNKS):
            if goes_far(way, c):
                ag_sent(r, way, half, c)
    rim.wait_send()
    for j in range(1, 2 * side):
        remote(st1.at[place], st1.at[place], st1_send.at[j], st1_recv.at[j], sibling).wait_send()
    for j in range(1, side):
        remote(st2.at[y], st2.at[y], st2_send.at[j], st2_recv.at[j], sibling).wait_send()

    def reduced(s, carry):
        for way in (RIGHT, LEFT):
            for c in range(CHUNKS):
                rs_copy(way, s, c).wait_send()
        return carry

    lax.fori_loop(2, half + 1, reduced, 0)
    for c in range(CHUNKS):
        rs_copy(RIGHT if goes_far(RIGHT, c) else LEFT, 1, c).wait_send()


def on_device(hidden, norm_gain, in_weight, short_weight, residues, rates, skip_gain, out_weight, lengths):
    samples, block, width = hidden.shape
    rows = in_weight.shape[0]
    n = lax.axis_size("tp")
    side = int(round(n ** 0.5))
    half = n // 2
    modes = rates.shape[0]
    dma = pltpu.SemaphoreType.DMA
    hbm = pl.BlockSpec(memory_space=pltpu.HBM)
    vmem = pl.BlockSpec(memory_space=pltpu.VMEM)
    state = (samples, modes, width)
    return pl.pallas_call(
        functools.partial(kernel, side),
        out_shape=jax.ShapeDtypeStruct((samples * block, width), BF16),
        in_specs=[hbm] * 8 + [pl.BlockSpec(memory_space=pltpu.SMEM)],
        out_specs=vmem,
        scratch_shapes=[
            pltpu.VMEM((1, n * width), F32),
            pltpu.VMEM(short_weight.shape, F32),
            pltpu.VMEM(rates.shape, F32),
            pltpu.VMEM(rates.shape, F32),
            pltpu.VMEM((1, width), F32),
            pltpu.VMEM((n, samples * block, width), BF16),
            pltpu.VMEM((samples * block, n * width), BF16),
            pltpu.VMEM((2 * n, rows, 3 * width + 2 * rows), BF16),
            pltpu.VMEM((samples * block, width // 2), F32),
            pltpu.VMEM((samples * block, 3 * width), F32),
            pltpu.VMEM((samples, block + 8, 3 * width), F32),
            pltpu.VMEM((samples, block, width), F32),
            pltpu.VMEM((samples, block, width), F32),
            pltpu.VMEM((samples, block, width), F32),
            pltpu.VMEM((samples * block, width), BF16),
            pltpu.VMEM((modes, block, width), F32),
            pltpu.VMEM(state, F32),
            pltpu.VMEM((2 * side,) + state, F32),
            pltpu.VMEM((side,) + state, F32),
            pltpu.VMEM((2, samples * block, width), F32),
            pltpu.VMEM((2, half, CHUNKS, samples * block // CHUNKS, width), BF16),
            pltpu.VMEM((2, half, CHUNKS, samples * block // CHUNKS, width), BF16),
            dma((11,)),
            dma((3, 2, half, CHUNKS)),
            dma((3, 2, half, CHUNKS)),
            dma((2, 2, half + 1)),
            dma((2, 2, half + 1)),
            dma,
            dma,
            dma((2 * side,)),
            dma((2 * side,)),
            dma((side,)),
            dma((side,)),
            dma((2, half, CHUNKS)),
            dma((2, half, CHUNKS)),
        ],
        compiler_params=pltpu.CompilerParams(
            collective_id=0, has_side_effects=True, vmem_limit_bytes=60 * 2**20
        ),
    )(
        hidden.reshape(samples * block, width),
        jnp.transpose(in_weight, (1, 0, 2)),
        out_weight,
        norm_gain.reshape(1, n * width),
        short_weight,
        residues,
        rates,
        skip_gain.reshape(1, width),
        lengths,
    ).reshape(hidden.shape)


def solution(mesh):
    placed = (
        P(None, "ctx", "tp"),
        P(),
        P("ctx", None, "tp"),
        P(None, None, "tp"),
        P(None, "tp"),
        P(None, "tp"),
        P("tp"),
        P("tp", "ctx"),
        P(),
    )
    return jax.shard_map(
        on_device, mesh=mesh, in_specs=placed, out_specs=P(None, "ctx", "tp"), check_vma=False
    )
```

```python
import functools

import jax
import jax.numpy as jnp
from jax import lax
from jax.experimental import pallas as pl
from jax.experimental.pallas import tpu as pltpu
from jax.sharding import PartitionSpec as P

MESH = pl.DeviceIdType.MESH
F32, BF16 = jnp.float32, jnp.bfloat16
RIGHT, LEFT = 0, 1
CHUNKS = 4


def rem(a, b):
    return lax.rem(a, jnp.int32(b))


def div(a, b):
    return lax.div(a, jnp.int32(b))


def remote(src, dst, send_sem, recv_sem, device):
    return pltpu.make_async_remote_copy(
        src_ref=src, dst_ref=dst, send_sem=send_sem, recv_sem=recv_sem,
        device_id=device, device_id_type=MESH,
    )


def kernel(
    side, hid_hbm, w_hbm, ow_hbm, gain_hbm, taps_hbm, res_hbm, rates_hbm, skip_hbm, len_ref, out_ref,
    gain_ref, taps_ref, res_ref, rates_ref, skip_ref,
    hraw, hs, pbuf, ssq, acc, ext, qbuf, ubuf, cbuf, gated, table, st_in, st1, st2, parts, rs_out, rs_in,
    load_sem, ag_send, ag_recv, sib_send, sib_recv, rim_send, rim_recv,
    st1_send, st1_recv, st2_send, st2_recv, rs_send, rs_recv,
):
    n = side * side
    half = n // 2
    samples, block, width = ubuf.shape
    rows = pbuf.shape[1]
    piece = samples * block // CHUNKS
    modes = rates_ref.shape[0]
    features = n * width
    me = lax.axis_index("ctx")
    z = lax.axis_index("tp")
    core = rem(me, 2)
    chip = div(me, 2)
    y, x = div(chip, side), rem(chip, side)
    turn = rem(x + y, side)
    sibling = {"ctx": me + 1 - 2 * core}

    def at(yy, xx):
        return {"ctx": 2 * (side * yy + xx) + core}

    place = rem(me, 2 * side)

    def in_row(steps):
        return {"ctx": me - place + rem(place + steps, 2 * side)}

    def chip_first(q):
        a = div(q, side)
        return side * a + rem(q - side * a + side - a, side)

    def chip_second(q):
        a = div(q, side)
        return side * rem(q - side * a + side - a, side) + a

    def from_last(steps):
        return rem(me + 2 * n - steps, 2 * n)

    quarter = rows // (2 * CHUNKS)
    first_place, second_place = side * y + turn, side * x + turn

    def ring(place, slot, device, chunk):
        return place, slot, chunk, (device(rem(place + 1, n)), device(rem(place + n - 1, n)))

    def first_slot(q):
        return 2 * chip_first(q) + core

    def second_slot(q):
        return 2 * chip_second(q) + core

    rings = [
        ring(z, lambda q: q, lambda q: {"tp": q}, lambda at_slot, c: hraw.at[at_slot, pl.ds(piece * c, piece)]),
        ring(
            first_place, first_slot, lambda q: {"ctx": first_slot(q)},
            lambda at_slot, c: pbuf.at[at_slot, pl.ds(quarter * c, quarter)],
        ),
        ring(
            second_place, second_slot, lambda q: {"ctx": second_slot(q)},
            lambda at_slot, c: pbuf.at[at_slot, pl.ds(rows // 2 + quarter * c, quarter)],
        ),
    ]

    def slot_of(r, way, s):
        spot, slot = rings[r][:2]
        return slot(rem(spot + n - s, n) if way == RIGHT else rem(spot + s, n))

    def ag_copy(r, way, s, c, at_slot):
        part = rings[r][2](at_slot, c)
        return remote(part, part, ag_send.at[r, way, s - 1, c], ag_recv.at[r, way, s - 1, c], rings[r][3][way])

    def ag_start(r, way, s, c, at_slot):
        ag_copy(r, way, s, c, at_slot).start()

    def ag_arrived(r, way, s, c):
        ag_copy(r, way, s, c, 0).wait_recv()

    def ag_sent(r, way, s, c):
        ag_copy(r, way, s, c, 0).wait_send()

    def sib_copy(r, way, s, at_slot):
        part = pbuf.at[at_slot, pl.ds(rows // 2 * (r - 1), rows // 2)]
        return remote(part, part, sib_send.at[r - 1, way, s], sib_recv.at[r - 1, way, s], sibling)

    def sib_wait(r, way, s):
        copy = sib_copy(r, way, s, 0)
        copy.wait_send()
        copy.wait_recv()

    loads = [pltpu.make_async_copy(hid_hbm, hraw.at[z], load_sem.at[0])]
    for j in range(3):
        loads.append(pltpu.make_async_copy(
            w_hbm.at[j], pbuf.at[me, :, pl.ds(width * j, width)], load_sem.at[1 + j]))
    for j in range(2):
        loads.append(pltpu.make_async_copy(
            ow_hbm.at[pl.ds(rows * j, rows)], pbuf.at[me, :, pl.ds(3 * width + rows * j, rows)], load_sem.at[4 + j]))
    small = [(gain_hbm, gain_ref), (taps_hbm, taps_ref), (res_hbm, res_ref), (rates_hbm, rates_ref), (skip_hbm, skip_ref)]
    for j, (source, target) in enumerate(small):
        loads.append(pltpu.make_async_copy(source, target, load_sem.at[6 + j]))
    for copy in loads:
        copy.start()
    partners = [{"tp": rem(z + 1, n)}, {"tp": rem(z + n - 1, n)}, {"ctx": from_last(1)}]
    partners += [in_row(j) for j in range(1, 2 * side)]
    partners += [at(rem(y + j, side), x) for j in range(1, side)]
    barrier = pltpu.get_barrier_semaphore()
    for partner in partners:
        pl.semaphore_signal(barrier, inc=1, device_id=partner, device_id_type=MESH)
    loads[0].wait()
    pl.semaphore_wait(barrier, len(partners))

    def take(q):
        gain = gain_ref[:, pl.ds(pl.multiple_of(q * width, width), width)]
        for s in range(samples):
            value = hraw[q, s * block : (s + 1) * block, :].astype(F32)
            span = pl.ds(s * block, block)
            square = value * value
            ssq[span, :] = ssq[span, :] + square[:, : width // 2] + square[:, width // 2 :]
            hs[span, pl.ds(pl.multiple_of(q * width, width), width)] = (value * gain).astype(BF16)

    def goes_far(way, c):
        return (c < CHUNKS // 2) == (way == RIGHT)

    lanes = [(r, way) for r in range(3) for way in (RIGHT, LEFT)]
    mine = [z, me, me]
    chunks = [(r, way, c if way == RIGHT else (c + CHUNKS // 2) % CHUNKS) for c in range(CHUNKS) for r, way in lanes]
    for r, way, c in chunks:
        if r == 0:
            ag_start(r, way, 1, c, mine[r])
    for copy in loads[1:]:
        copy.wait()
    for r, way, c in chunks:
        if r:
            ag_start(r, way, 1, c, mine[r])
    for r in (1, 2):
        sib_copy(r, RIGHT, 0, me).start()
    ssq[...] = jnp.zeros_like(ssq)
    take(z)

    def ag_step(s, carry):
        slots = {(r, way): slot_of(r, way, s) for r, way in lanes}
        for r, way, c in chunks:
            ag_arrived(r, way, s, c)
            ag_start(r, way, s + 1, c, slots[r, way])
        for r, way in lanes[2:]:
            sib_copy(r, way, s, slots[r, way]).start()
        take(slots[0, RIGHT])
        take(slots[0, LEFT])
        return carry

    lax.fori_loop(1, half - 1, ag_step, 0)
    slots = {(r, way): slot_of(r, way, half - 1) for r, way in lanes}
    for r, way, c in chunks:
        ag_arrived(r, way, half - 1, c)
        if goes_far(way, c):
            ag_start(r, way, half, c, slots[r, way])
    for r, way in lanes[2:]:
        sib_copy(r, way, half - 1, slots[r, way]).start()
    take(slots[0, RIGHT])
    take(slots[0, LEFT])
    for r in (1, 2, 0):
        for c in range(CHUNKS):
            ag_arrived(r, RIGHT if goes_far(RIGHT, c) else LEFT, half, c)
        if r:
            sib_copy(r, RIGHT, half, slot_of(r, RIGHT, half)).start()
    take(slot_of(0, RIGHT, half))
    for r in (1, 2):
        sib_wait(r, RIGHT, 0)

    def sib_step(s, carry):
        for r in (1, 2):
            for way in (RIGHT, LEFT):
                sib_wait(r, way, s)
        return carry

    lax.fori_loop(1, half, sib_step, 0)

    span_k = side * width
    per = span_k // rows

    def product(steps):
        i = rem(y + steps, side)
        left = hs[:, pl.ds(pl.multiple_of(i * span_k, span_k), span_k)]
        right = pbuf[pl.ds(i * per, per), :, : 3 * width].reshape(span_k, 3 * width)
        return jnp.dot(left, right, preferred_element_type=F32)

    acc[...] = product(0)
    for steps in range(1, side):
        if steps != side // 2:
            acc[...] = acc[...] + product(steps)
    for r in (1, 2):
        sib_wait(r, RIGHT, half)
    acc[...] = acc[...] + product(side // 2)
    mean = jnp.sum(ssq[...], axis=1, keepdims=True) * (1.0 / features)
    scale = lax.rsqrt(mean + 1e-6)
    for s in range(samples):
        ext[s, 8:, :] = acc[s * block : (s + 1) * block, :] * scale[s * block : (s + 1) * block, :]
    rim = remote(ext.at[:, pl.ds(block, 8)], ext.at[:, pl.ds(0, 8)], rim_send, rim_recv, {"ctx": rem(me + 1, 2 * n)})
    rim.start()

    rates = rates_ref[...]
    decay = jnp.exp(-rates)
    coef = res_ref[...] * jnp.sqrt(2.0 * rates / modes)

    def powers(spot, blocks, count):
        before, total = [], []
        for i in range(count):
            gap = jnp.maximum(spot - 1 - i, 0).astype(F32)
            factor = jnp.exp(-rates * (gap * float(blocks * block)))
            before.append(jnp.where(i < spot, factor, 0.0))
            total.append(jnp.exp(-rates * float(blocks * block * (count - 1 - i))))
        return before, total

    def filtered(s, j, first, count):
        total = None
        for i in range(3):
            term = taps_ref[i, j : j + 1, :] * ext[s, 8 + first - i : 8 + first - i + count, j * width : (j + 1) * width]
            total = term if total is None else total + term
        return total

    def features_of(first, count):
        for s in range(samples):
            position = lax.broadcasted_iota(jnp.int32, (count, 1), 0) + (me * block + first)
            valid = jnp.where(position < len_ref[s], 1.0, 0.0)
            span = slice(first, first + count)
            pushed = filtered(s, 1, first, count) * filtered(s, 2, first, count) * valid
            ubuf[s, span, :] = pushed.astype(BF16).astype(F32)
            qbuf[s, span, :] = filtered(s, 0, first, count) * valid

    def gather_state(g, states):
        states = list(states)
        tiles = [ubuf[s, pl.ds(pl.multiple_of(8 * g, 8), 8), :] for s in range(samples)]
        for i in range(8):
            for s in range(samples):
                states[s] = decay * states[s] + tiles[s][i : i + 1, :]
        return tuple(states)

    zero = jnp.zeros((modes, width), F32)
    features_of(8, block - 8)
    ends = lax.fori_loop(1, block // 8, gather_state, (zero,) * samples)
    rim.wait_recv()
    for s in range(samples):
        ext[s, :8, :] = jnp.where(me == 0, 0.0, ext[s, :8, :])
    features_of(0, 8)
    heads = gather_state(0, (zero,) * samples)
    late = jnp.exp(-rates * float(block - 8))
    for s in range(samples):
        st1[place, s] = late * heads[s] + ends[s]
    for j in range(1, 2 * side):
        remote(st1.at[place], st1.at[place], st1_send.at[j], st1_recv.at[j], in_row(j)).start()

    def fill_table(m, carry):
        rate = rates_ref[pl.ds(m, 1), :]
        steps = lax.broadcasted_iota(jnp.int32, (block, 1), 0).astype(F32) + 1.0
        table[m] = res_ref[pl.ds(m, 1), :] * jnp.sqrt(2.0 * rate / modes) * jnp.exp(-rate * steps)
        return carry

    def convolve(s):
        def body(g, state):
            span = pl.ds(pl.multiple_of(8 * g, 8), 8)
            tile = ubuf[s, span, :]
            lines = []
            for i in range(8):
                state = decay * state + tile[i : i + 1, :]
                lines.append(jnp.sum(coef * state, axis=0, keepdims=True))
            cbuf[s, span, :] = jnp.concatenate(lines, axis=0)
            return state

        lax.fori_loop(0, block // 8, body, zero)

    x_before, x_total = powers(place, 1, 2 * side)
    lax.fori_loop(0, modes, fill_table, 0)
    convolve(0)
    for j in range(1, 2 * side):
        slot = st1.at[rem(place + 2 * side - j, 2 * side)]
        remote(slot, slot, st1_send.at[j], st1_recv.at[j], sibling).wait_recv()
    for s in range(samples):
        st2[y, s] = sum(x_total[i] * st1[i, s] for i in range(2 * side))
    for j in range(1, side):
        remote(st2.at[y], st2.at[y], st2_send.at[j], st2_recv.at[j], at(rem(y + j, side), x)).start()
    y_before, _ = powers(y, 2 * side, side)
    x_power = jnp.exp(-rates * (place.astype(F32) * float(block)))
    convolve(1)
    for j in range(1, side):
        slot = st2.at[rem(y + side - j, side)]
        remote(slot, slot, st2_send.at[j], st2_recv.at[j], sibling).wait_recv()
    for s in range(samples):
        row = sum(y_before[i] * st2[i, s] for i in range(side))
        st_in[s] = x_power * row + sum(x_before[i] * st1[i, s] for i in range(2 * side))

    tall = 32

    def carry_in(g, carry):
        span = pl.ds(pl.multiple_of(tall * g, tall), tall)
        totals = [cbuf[s, span, :] + skip_ref[...] * ubuf[s, span, :] for s in range(samples)]
        for m in range(modes):
            weight = table[m, span, :]
            for s in range(samples):
                totals[s] = totals[s] + weight * st_in[s, m : m + 1, :]
        for s in range(samples):
            target = pl.ds(pl.multiple_of(block * s + tall * g, tall), tall)
            gated[target, :] = (qbuf[s, span, :] * totals[s]).astype(BF16)
        return carry

    lax.fori_loop(0, block // tall, carry_in, 0)

    def share(d):
        first, second = pbuf[2 * d, :, 3 * width :], pbuf[2 * d + 1, :, 3 * width :]
        right = jnp.concatenate([
            jnp.concatenate([first[:, :rows], second[:, :rows]], axis=1),
            jnp.concatenate([first[:, rows:], second[:, rows:]], axis=1),
        ], axis=0)
        return jnp.dot(gated[...], right, preferred_element_type=F32)

    def rs_copy(way, s, c):
        return remote(
            rs_out.at[way, s - 1, c], rs_in.at[way, s - 1, c],
            rs_send.at[way, s - 1, c], rs_recv.at[way, s - 1, c], rings[0][3][way],
        )

    def prepare(s):
        ahead = half + 1 - s
        parts[RIGHT] = share(rem(z + ahead, n))
        parts[LEFT] = share(rem(z + n - ahead, n))

    def rs_step(s, way, c, first):
        part = parts[way, piece * c : piece * (c + 1), :]
        if not first:
            rs_copy(way, s - 1, c).wait_recv()
            part = part + rs_in[way, s - 2, c].astype(F32)
        rs_out[way, s - 1, c] = part.astype(BF16)
        rs_copy(way, s, c).start()

    order = [(way, c) for far in (False, True) for c in range(CHUNKS) for way in (RIGHT, LEFT) if goes_far(way, c) == far]
    farthest = share(rem(z + half, n))
    for c in range(CHUNKS):
        way = RIGHT if goes_far(RIGHT, c) else LEFT
        rs_out[way, 0, c] = farthest[piece * c : piece * (c + 1), :].astype(BF16)
        rs_copy(way, 1, c).start()
    prepare(2)
    for way, c in order:
        rs_step(2, way, c, not goes_far(way, c))

    def reduce_step(s, carry):
        prepare(s)
        for way, c in order:
            rs_step(s, way, c, False)
        return carry

    lax.fori_loop(3, half + 1, reduce_step, 0)
    own = share(z)
    for c in range(CHUNKS):
        span = slice(piece * c, piece * (c + 1))
        part = own[span, :] + hraw[z, span, :].astype(F32)
        for way in (RIGHT, LEFT):
            rs_copy(way, half, c).wait_recv()
            part = part + rs_in[way, half - 1, c].astype(F32)
        out_ref[span, :] = part.astype(BF16)

    def sent(s, carry):
        for r, way in lanes:
            for c in range(CHUNKS):
                ag_sent(r, way, s, c)
        return carry

    lax.fori_loop(1, half, sent, 0)
    for r, way in lanes:
        for c in range(CHUNKS):
            if goes_far(way, c):
                ag_sent(r, way, half, c)
    rim.wait_send()
    for j in range(1, 2 * side):
        remote(st1.at[place], st1.at[place], st1_send.at[j], st1_recv.at[j], sibling).wait_send()
    for j in range(1, side):
        remote(st2.at[y], st2.at[y], st2_send.at[j], st2_recv.at[j], sibling).wait_send()

    def reduced(s, carry):
        for way in (RIGHT, LEFT):
            for c in range(CHUNKS):
                rs_copy(way, s, c).wait_send()
        return carry

    lax.fori_loop(2, half + 1, reduced, 0)
    for c in range(CHUNKS):
        rs_copy(RIGHT if goes_far(RIGHT, c) else LEFT, 1, c).wait_send()


def on_device(hidden, norm_gain, in_weight, short_weight, residues, rates, skip_gain, out_weight, lengths):
    samples, block, width = hidden.shape
    rows = in_weight.shape[0]
    n = lax.axis_size("tp")
    side = int(round(n ** 0.5))
    half = n // 2
    modes = rates.shape[0]
    dma = pltpu.SemaphoreType.DMA
    hbm = pl.BlockSpec(memory_space=pltpu.HBM)
    vmem = pl.BlockSpec(memory_space=pltpu.VMEM)
    state = (samples, modes, width)
    return pl.pallas_call(
        functools.partial(kernel, side),
        out_shape=jax.ShapeDtypeStruct((samples * block, width), BF16),
        in_specs=[hbm] * 8 + [pl.BlockSpec(memory_space=pltpu.SMEM)],
        out_specs=vmem,
        scratch_shapes=[
            pltpu.VMEM((1, n * width), F32),
            pltpu.VMEM(short_weight.shape, F32),
            pltpu.VMEM(rates.shape, F32),
            pltpu.VMEM(rates.shape, F32),
            pltpu.VMEM((1, width), F32),
            pltpu.VMEM((n, samples * block, width), BF16),
            pltpu.VMEM((samples * block, n * width), BF16),
            pltpu.VMEM((2 * n, rows, 3 * width + 2 * rows), BF16),
            pltpu.VMEM((samples * block, width // 2), F32),
            pltpu.VMEM((samples * block, 3 * width), F32),
            pltpu.VMEM((samples, block + 8, 3 * width), F32),
            pltpu.VMEM((samples, block, width), F32),
            pltpu.VMEM((samples, block, width), F32),
            pltpu.VMEM((samples, block, width), F32),
            pltpu.VMEM((samples * block, width), BF16),
            pltpu.VMEM((modes, block, width), F32),
            pltpu.VMEM(state, F32),
            pltpu.VMEM((2 * side,) + state, F32),
            pltpu.VMEM((side,) + state, F32),
            pltpu.VMEM((2, samples * block, width), F32),
            pltpu.VMEM((2, half, CHUNKS, samples * block // CHUNKS, width), BF16),
            pltpu.VMEM((2, half, CHUNKS, samples * block // CHUNKS, width), BF16),
            dma((11,)),
            dma((3, 2, half, CHUNKS)),
            dma((3, 2, half, CHUNKS)),
            dma((2, 2, half + 1)),
            dma((2, 2, half + 1)),
            dma,
            dma,
            dma((2 * side,)),
            dma((2 * side,)),
            dma((side,)),
            dma((side,)),
            dma((2, half, CHUNKS)),
            dma((2, half, CHUNKS)),
        ],
        compiler_params=pltpu.CompilerParams(
            collective_id=0, has_side_effects=True, vmem_limit_bytes=60 * 2**20
        ),
    )(
        hidden.reshape(samples * block, width),
        jnp.transpose(in_weight, (1, 0, 2)),
        out_weight,
        norm_gain.reshape(1, n * width),
        short_weight,
        residues,
        rates,
        skip_gain.reshape(1, width),
        lengths,
    ).reshape(hidden.shape)


def solution(mesh):
    placed = (
        P(None, "ctx", "tp"),
        P(),
        P("ctx", None, "tp"),
        P(None, None, "tp"),
        P(None, "tp"),
        P(None, "tp"),
        P("tp"),
        P("tp", "ctx"),
        P(),
    )
    return jax.shard_map(
        on_device, mesh=mesh, in_specs=placed, out_specs=P(None, "ctx", "tp"), check_vma=False
    )
```

```python
import functools

import jax
import jax.numpy as jnp
from jax import lax
from jax.experimental import pallas as pl
from jax.experimental.pallas import tpu as pltpu
from jax.sharding import PartitionSpec as P

MESH = pl.DeviceIdType.MESH
F32, BF16 = jnp.float32, jnp.bfloat16
RIGHT, LEFT = 0, 1
CHUNKS = 4


def rem(a, b):
    return lax.rem(a, jnp.int32(b))


def div(a, b):
    return lax.div(a, jnp.int32(b))


def remote(src, dst, send_sem, recv_sem, device):
    return pltpu.make_async_remote_copy(
        src_ref=src, dst_ref=dst, send_sem=send_sem, recv_sem=recv_sem,
        device_id=device, device_id_type=MESH,
    )


def kernel(
    side, hid_hbm, w_hbm, ow_hbm, gain_hbm, taps_hbm, res_hbm, rates_hbm, skip_hbm, len_ref, out_ref,
    gain_ref, taps_ref, res_ref, rates_ref, skip_ref,
    hraw, hs, pbuf, ssq, acc, ext, qbuf, ubuf, cbuf, gated, table, st_in, st1, st2, parts, rs_out, rs_in,
    load_sem, ag_send, ag_recv, sib_send, sib_recv, rim_send, rim_recv,
    st1_send, st1_recv, st2_send, st2_recv, rs_send, rs_recv,
):
    n = side * side
    half = n // 2
    samples, block, width = ubuf.shape
    rows = pbuf.shape[1]
    piece = samples * block // CHUNKS
    modes = rates_ref.shape[0]
    features = n * width
    me = lax.axis_index("ctx")
    z = lax.axis_index("tp")
    core = rem(me, 2)
    chip = div(me, 2)
    y, x = div(chip, side), rem(chip, side)
    turn = rem(x + y, side)
    sibling = {"ctx": me + 1 - 2 * core}

    def at(yy, xx):
        return {"ctx": 2 * (side * yy + xx) + core}

    place = rem(me, 2 * side)

    def in_row(steps):
        return {"ctx": me - place + rem(place + steps, 2 * side)}

    def chip_first(q):
        a = div(q, side)
        return side * a + rem(q - side * a + side - a, side)

    def chip_second(q):
        a = div(q, side)
        return side * rem(q - side * a + side - a, side) + a

    def from_last(steps):
        return rem(me + 2 * n - steps, 2 * n)

    quarter = rows // (2 * CHUNKS)
    first_place, second_place = side * y + turn, side * x + turn

    def ring(place, slot, device, chunk):
        return place, slot, chunk, (device(rem(place + 1, n)), device(rem(place + n - 1, n)))

    def first_slot(q):
        return 2 * chip_first(q) + core

    def second_slot(q):
        return 2 * chip_second(q) + core

    rings = [
        ring(z, lambda q: q, lambda q: {"tp": q}, lambda at_slot, c: hraw.at[at_slot, pl.ds(piece * c, piece)]),
        ring(
            first_place, first_slot, lambda q: {"ctx": first_slot(q)},
            lambda at_slot, c: pbuf.at[at_slot, pl.ds(quarter * c, quarter)],
        ),
        ring(
            second_place, second_slot, lambda q: {"ctx": second_slot(q)},
            lambda at_slot, c: pbuf.at[at_slot, pl.ds(rows // 2 + quarter * c, quarter)],
        ),
    ]

    def slot_of(r, way, s):
        spot, slot = rings[r][:2]
        return slot(rem(spot + n - s, n) if way == RIGHT else rem(spot + s, n))

    def ag_copy(r, way, s, c, at_slot):
        part = rings[r][2](at_slot, c)
        return remote(part, part, ag_send.at[r, way, s - 1, c], ag_recv.at[r, way, s - 1, c], rings[r][3][way])

    def ag_start(r, way, s, c, at_slot):
        ag_copy(r, way, s, c, at_slot).start()

    def ag_arrived(r, way, s, c):
        ag_copy(r, way, s, c, 0).wait_recv()

    def ag_sent(r, way, s, c):
        ag_copy(r, way, s, c, 0).wait_send()

    def sib_copy(r, way, s, at_slot):
        part = pbuf.at[at_slot, pl.ds(rows // 2 * (r - 1), rows // 2)]
        return remote(part, part, sib_send.at[r - 1, way, s], sib_recv.at[r - 1, way, s], sibling)

    def sib_wait(r, way, s):
        copy = sib_copy(r, way, s, 0)
        copy.wait_send()
        copy.wait_recv()

    loads = [pltpu.make_async_copy(hid_hbm, hraw.at[z], load_sem.at[0])]
    for j in range(3):
        loads.append(pltpu.make_async_copy(
            w_hbm.at[j], pbuf.at[me, :, pl.ds(width * j, width)], load_sem.at[1 + j]))
    for j in range(2):
        loads.append(pltpu.make_async_copy(
            ow_hbm.at[pl.ds(rows * j, rows)], pbuf.at[me, :, pl.ds(3 * width + rows * j, rows)], load_sem.at[4 + j]))
    small = [(gain_hbm, gain_ref), (taps_hbm, taps_ref), (res_hbm, res_ref), (rates_hbm, rates_ref), (skip_hbm, skip_ref)]
    for j, (source, target) in enumerate(small):
        loads.append(pltpu.make_async_copy(source, target, load_sem.at[6 + j]))
    for copy in loads:
        copy.start()
    partners = [{"tp": rem(z + 1, n)}, {"tp": rem(z + n - 1, n)}, {"ctx": from_last(1)}]
    partners += [in_row(j) for j in range(1, 2 * side)]
    partners += [at(rem(y + j, side), x) for j in range(1, side)]
    barrier = pltpu.get_barrier_semaphore()
    for partner in partners:
        pl.semaphore_signal(barrier, inc=1, device_id=partner, device_id_type=MESH)
    loads[0].wait()
    pl.semaphore_wait(barrier, len(partners))

    def take(q):
        gain = gain_ref[:, pl.ds(pl.multiple_of(q * width, width), width)]
        for s in range(samples):
            value = hraw[q, s * block : (s + 1) * block, :].astype(F32)
            span = pl.ds(s * block, block)
            square = value * value
            ssq[span, :] = ssq[span, :] + square[:, : width // 2] + square[:, width // 2 :]
            hs[span, pl.ds(pl.multiple_of(q * width, width), width)] = (value * gain).astype(BF16)

    def goes_far(way, c):
        return (c < CHUNKS // 2) == (way == RIGHT)

    lanes = [(r, way) for r in range(3) for way in (RIGHT, LEFT)]
    mine = [z, me, me]
    chunks = [(r, way, c if way == RIGHT else (c + CHUNKS // 2) % CHUNKS) for c in range(CHUNKS) for r, way in lanes[2:] + lanes[:2]]
    for r, way, c in chunks:
        if r == 0:
            ag_start(r, way, 1, c, mine[r])
    for copy in loads[1:]:
        copy.wait()
    for r, way, c in chunks:
        if r:
            ag_start(r, way, 1, c, mine[r])
    for r in (1, 2):
        sib_copy(r, RIGHT, 0, me).start()
    ssq[...] = jnp.zeros_like(ssq)
    take(z)

    def ag_step(s, carry):
        slots = {(r, way): slot_of(r, way, s) for r, way in lanes}
        for r, way, c in chunks:
            ag_arrived(r, way, s, c)
            ag_start(r, way, s + 1, c, slots[r, way])
        for r, way in lanes[2:]:
            sib_copy(r, way, s, slots[r, way]).start()
        take(slots[0, RIGHT])
        take(slots[0, LEFT])
        return carry

    lax.fori_loop(1, half - 1, ag_step, 0)
    slots = {(r, way): slot_of(r, way, half - 1) for r, way in lanes}
    for r, way, c in chunks:
        ag_arrived(r, way, half - 1, c)
        if goes_far(way, c):
            ag_start(r, way, half, c, slots[r, way])
    for r, way in lanes[2:]:
        sib_copy(r, way, half - 1, slots[r, way]).start()
    take(slots[0, RIGHT])
    take(slots[0, LEFT])
    for r in (1, 2, 0):
        for c in range(CHUNKS):
            ag_arrived(r, RIGHT if goes_far(RIGHT, c) else LEFT, half, c)
        if r:
            sib_copy(r, RIGHT, half, slot_of(r, RIGHT, half)).start()
    take(slot_of(0, RIGHT, half))
    for r in (1, 2):
        sib_wait(r, RIGHT, 0)

    def sib_step(s, carry):
        for r in (1, 2):
            for way in (RIGHT, LEFT):
                sib_wait(r, way, s)
        return carry

    lax.fori_loop(1, half, sib_step, 0)

    span_k = side * width
    per = span_k // rows

    def product(steps):
        i = rem(y + steps, side)
        left = hs[:, pl.ds(pl.multiple_of(i * span_k, span_k), span_k)]
        right = pbuf[pl.ds(i * per, per), :, : 3 * width].reshape(span_k, 3 * width)
        return jnp.dot(left, right, preferred_element_type=F32)

    acc[...] = product(0)
    for steps in range(1, side):
        if steps != side // 2:
            acc[...] = acc[...] + product(steps)
    for r in (1, 2):
        sib_wait(r, RIGHT, half)
    acc[...] = acc[...] + product(side // 2)
    mean = jnp.sum(ssq[...], axis=1, keepdims=True) * (1.0 / features)
    scale = lax.rsqrt(mean + 1e-6)
    for s in range(samples):
        ext[s, 8:, :] = acc[s * block : (s + 1) * block, :] * scale[s * block : (s + 1) * block, :]
    rim = remote(ext.at[:, pl.ds(block, 8)], ext.at[:, pl.ds(0, 8)], rim_send, rim_recv, {"ctx": rem(me + 1, 2 * n)})
    rim.start()

    rates = rates_ref[...]
    decay = jnp.exp(-rates)
    coef = res_ref[...] * jnp.sqrt(2.0 * rates / modes)

    def powers(spot, blocks, count):
        before, total = [], []
        for i in range(count):
            gap = jnp.maximum(spot - 1 - i, 0).astype(F32)
            factor = jnp.exp(-rates * (gap * float(blocks * block)))
            before.append(jnp.where(i < spot, factor, 0.0))
            total.append(jnp.exp(-rates * float(blocks * block * (count - 1 - i))))
        return before, total

    def filtered(s, j, first, count):
        total = None
        for i in range(3):
            term = taps_ref[i, j : j + 1, :] * ext[s, 8 + first - i : 8 + first - i + count, j * width : (j + 1) * width]
            total = term if total is None else total + term
        return total

    def features_of(first, count):
        for s in range(samples):
            position = lax.broadcasted_iota(jnp.int32, (count, 1), 0) + (me * block + first)
            valid = jnp.where(position < len_ref[s], 1.0, 0.0)
            span = slice(first, first + count)
            pushed = filtered(s, 1, first, count) * filtered(s, 2, first, count) * valid
            ubuf[s, span, :] = pushed.astype(BF16).astype(F32)
            qbuf[s, span, :] = filtered(s, 0, first, count) * valid

    def gather_state(g, states):
        states = list(states)
        tiles = [ubuf[s, pl.ds(pl.multiple_of(8 * g, 8), 8), :] for s in range(samples)]
        for i in range(8):
            for s in range(samples):
                states[s] = decay * states[s] + tiles[s][i : i + 1, :]
        return tuple(states)

    zero = jnp.zeros((modes, width), F32)
    features_of(8, block - 8)
    ends = lax.fori_loop(1, block // 8, gather_state, (zero,) * samples)
    rim.wait_recv()
    for s in range(samples):
        ext[s, :8, :] = jnp.where(me == 0, 0.0, ext[s, :8, :])
    features_of(0, 8)
    heads = gather_state(0, (zero,) * samples)
    late = jnp.exp(-rates * float(block - 8))
    for s in range(samples):
        st1[place, s] = late * heads[s] + ends[s]
    for j in range(1, 2 * side):
        remote(st1.at[place], st1.at[place], st1_send.at[j], st1_recv.at[j], in_row(j)).start()

    def fill_table(m, carry):
        rate = rates_ref[pl.ds(m, 1), :]
        steps = lax.broadcasted_iota(jnp.int32, (block, 1), 0).astype(F32) + 1.0
        table[m] = res_ref[pl.ds(m, 1), :] * jnp.sqrt(2.0 * rate / modes) * jnp.exp(-rate * steps)
        return carry

    def convolve(s):
        def body(g, state):
            span = pl.ds(pl.multiple_of(8 * g, 8), 8)
            tile = ubuf[s, span, :]
            lines = []
            for i in range(8):
                state = decay * state + tile[i : i + 1, :]
                lines.append(jnp.sum(coef * state, axis=0, keepdims=True))
            cbuf[s, span, :] = jnp.concatenate(lines, axis=0)
            return state

        lax.fori_loop(0, block // 8, body, zero)

    x_before, x_total = powers(place, 1, 2 * side)
    lax.fori_loop(0, modes, fill_table, 0)
    convolve(0)
    for j in range(1, 2 * side):
        slot = st1.at[rem(place + 2 * side - j, 2 * side)]
        remote(slot, slot, st1_send.at[j], st1_recv.at[j], sibling).wait_recv()
    for s in range(samples):
        st2[y, s] = sum(x_total[i] * st1[i, s] for i in range(2 * side))
    for j in range(1, side):
        remote(st2.at[y], st2.at[y], st2_send.at[j], st2_recv.at[j], at(rem(y + j, side), x)).start()
    y_before, _ = powers(y, 2 * side, side)
    x_power = jnp.exp(-rates * (place.astype(F32) * float(block)))
    convolve(1)
    for j in range(1, side):
        slot = st2.at[rem(y + side - j, side)]
        remote(slot, slot, st2_send.at[j], st2_recv.at[j], sibling).wait_recv()
    for s in range(samples):
        row = sum(y_before[i] * st2[i, s] for i in range(side))
        st_in[s] = x_power * row + sum(x_before[i] * st1[i, s] for i in range(2 * side))

    tall = 32

    def carry_in(g, carry):
        span = pl.ds(pl.multiple_of(tall * g, tall), tall)
        totals = [cbuf[s, span, :] + skip_ref[...] * ubuf[s, span, :] for s in range(samples)]
        for m in range(modes):
            weight = table[m, span, :]
            for s in range(samples):
                totals[s] = totals[s] + weight * st_in[s, m : m + 1, :]
        for s in range(samples):
            target = pl.ds(pl.multiple_of(block * s + tall * g, tall), tall)
            gated[target, :] = (qbuf[s, span, :] * totals[s]).astype(BF16)
        return carry

    lax.fori_loop(0, block // tall, carry_in, 0)

    def share(d):
        first, second = pbuf[2 * d, :, 3 * width :], pbuf[2 * d + 1, :, 3 * width :]
        right = jnp.concatenate([
            jnp.concatenate([first[:, :rows], second[:, :rows]], axis=1),
            jnp.concatenate([first[:, rows:], second[:, rows:]], axis=1),
        ], axis=0)
        return jnp.dot(gated[...], right, preferred_element_type=F32)

    def rs_copy(way, s, c):
        return remote(
            rs_out.at[way, s - 1, c], rs_in.at[way, s - 1, c],
            rs_send.at[way, s - 1, c], rs_recv.at[way, s - 1, c], rings[0][3][way],
        )

    def prepare(s):
        ahead = half + 1 - s
        parts[RIGHT] = share(rem(z + ahead, n))
        parts[LEFT] = share(rem(z + n - ahead, n))

    def rs_step(s, way, c, first):
        part = parts[way, piece * c : piece * (c + 1), :]
        if not first:
            rs_copy(way, s - 1, c).wait_recv()
            part = part + rs_in[way, s - 2, c].astype(F32)
        rs_out[way, s - 1, c] = part.astype(BF16)
        rs_copy(way, s, c).start()

    order = [(way, c) for far in (False, True) for c in range(CHUNKS) for way in (RIGHT, LEFT) if goes_far(way, c) == far]
    farthest = share(rem(z + half, n))
    for c in range(CHUNKS):
        way = RIGHT if goes_far(RIGHT, c) else LEFT
        rs_out[way, 0, c] = farthest[piece * c : piece * (c + 1), :].astype(BF16)
        rs_copy(way, 1, c).start()
    prepare(2)
    for way, c in order:
        rs_step(2, way, c, not goes_far(way, c))

    def reduce_step(s, carry):
        prepare(s)
        for way, c in order:
            rs_step(s, way, c, False)
        return carry

    lax.fori_loop(3, half + 1, reduce_step, 0)
    own = share(z)
    for c in range(CHUNKS):
        span = slice(piece * c, piece * (c + 1))
        part = own[span, :] + hraw[z, span, :].astype(F32)
        for way in (RIGHT, LEFT):
            rs_copy(way, half, c).wait_recv()
            part = part + rs_in[way, half - 1, c].astype(F32)
        out_ref[span, :] = part.astype(BF16)

    def sent(s, carry):
        for r, way in lanes:
            for c in range(CHUNKS):
                ag_sent(r, way, s, c)
        return carry

    lax.fori_loop(1, half, sent, 0)
    for r, way in lanes:
        for c in range(CHUNKS):
            if goes_far(way, c):
                ag_sent(r, way, half, c)
    rim.wait_send()
    for j in range(1, 2 * side):
        remote(st1.at[place], st1.at[place], st1_send.at[j], st1_recv.at[j], sibling).wait_send()
    for j in range(1, side):
        remote(st2.at[y], st2.at[y], st2_send.at[j], st2_recv.at[j], sibling).wait_send()

    def reduced(s, carry):
        for way in (RIGHT, LEFT):
            for c in range(CHUNKS):
                rs_copy(way, s, c).wait_send()
        return carry

    lax.fori_loop(2, half + 1, reduced, 0)
    for c in range(CHUNKS):
        rs_copy(RIGHT if goes_far(RIGHT, c) else LEFT, 1, c).wait_send()


def on_device(hidden, norm_gain, in_weight, short_weight, residues, rates, skip_gain, out_weight, lengths):
    samples, block, width = hidden.shape
    rows = in_weight.shape[0]
    n = lax.axis_size("tp")
    side = int(round(n ** 0.5))
    half = n // 2
    modes = rates.shape[0]
    dma = pltpu.SemaphoreType.DMA
    hbm = pl.BlockSpec(memory_space=pltpu.HBM)
    vmem = pl.BlockSpec(memory_space=pltpu.VMEM)
    state = (samples, modes, width)
    return pl.pallas_call(
        functools.partial(kernel, side),
        out_shape=jax.ShapeDtypeStruct((samples * block, width), BF16),
        in_specs=[hbm] * 8 + [pl.BlockSpec(memory_space=pltpu.SMEM)],
        out_specs=vmem,
        scratch_shapes=[
            pltpu.VMEM((1, n * width), F32),
            pltpu.VMEM(short_weight.shape, F32),
            pltpu.VMEM(rates.shape, F32),
            pltpu.VMEM(rates.shape, F32),
            pltpu.VMEM((1, width), F32),
            pltpu.VMEM((n, samples * block, width), BF16),
            pltpu.VMEM((samples * block, n * width), BF16),
            pltpu.VMEM((2 * n, rows, 3 * width + 2 * rows), BF16),
            pltpu.VMEM((samples * block, width // 2), F32),
            pltpu.VMEM((samples * block, 3 * width), F32),
            pltpu.VMEM((samples, block + 8, 3 * width), F32),
            pltpu.VMEM((samples, block, width), F32),
            pltpu.VMEM((samples, block, width), F32),
            pltpu.VMEM((samples, block, width), F32),
            pltpu.VMEM((samples * block, width), BF16),
            pltpu.VMEM((modes, block, width), F32),
            pltpu.VMEM(state, F32),
            pltpu.VMEM((2 * side,) + state, F32),
            pltpu.VMEM((side,) + state, F32),
            pltpu.VMEM((2, samples * block, width), F32),
            pltpu.VMEM((2, half, CHUNKS, samples * block // CHUNKS, width), BF16),
            pltpu.VMEM((2, half, CHUNKS, samples * block // CHUNKS, width), BF16),
            dma((11,)),
            dma((3, 2, half, CHUNKS)),
            dma((3, 2, half, CHUNKS)),
            dma((2, 2, half + 1)),
            dma((2, 2, half + 1)),
            dma,
            dma,
            dma((2 * side,)),
            dma((2 * side,)),
            dma((side,)),
            dma((side,)),
            dma((2, half, CHUNKS)),
            dma((2, half, CHUNKS)),
        ],
        compiler_params=pltpu.CompilerParams(
            collective_id=0, has_side_effects=True, vmem_limit_bytes=60 * 2**20
        ),
    )(
        hidden.reshape(samples * block, width),
        jnp.transpose(in_weight, (1, 0, 2)),
        out_weight,
        norm_gain.reshape(1, n * width),
        short_weight,
        residues,
        rates,
        skip_gain.reshape(1, width),
        lengths,
    ).reshape(hidden.shape)


def solution(mesh):
    placed = (
        P(None, "ctx", "tp"),
        P(),
        P("ctx", None, "tp"),
        P(None, None, "tp"),
        P(None, "tp"),
        P(None, "tp"),
        P("tp"),
        P("tp", "ctx"),
        P(),
    )
    return jax.shard_map(
        on_device, mesh=mesh, in_specs=placed, out_specs=P(None, "ctx", "tp"), check_vma=False
    )
```
